256 devices in a mesh: ctx: 32 (over z, x), head: 8 (over y, core).
Axes of the slice: x: 4, y: 4, z: 8, core: 2. Of those that a mesh axis runs over, the one named last changes fastest.
Arguments:
- queries: bfloat16 [256, 128, 128], P('head'), may hold values from -48 to 48
- keys: bfloat16 [8, 262144, 128], P('head', 'ctx'), may hold values from -6 to 6
- values: bfloat16 [8, 262144, 128], P('head', 'ctx'), may hold values from -6 to 6
- key_block_scale: float32 [8, 4096], P('head', 'ctx'), may hold values from 0.5 to 2
- value_block_scale: float32 [8, 4096], P('head', 'ctx'), may hold values from 0.5 to 2
- selection: int32 [8, 512], P('head'), may hold values from 0 to 4095, as said below
Outputs:
- attended: bfloat16 [256, 128, 128], P('ctx', 'head')
The draws below stay inside these ranges and needn't reach their ends.
Inputs may be any that keep to these rules, and one draw needn't show every extreme that they name: `selection`: each row lists 512 distinct block numbers in increasing order. Of the blocks i * 128 to (i + 1) * 128 - 1, a row lists between 1 and 40, and exactly 40 for some i in every row.
All inputs are finite; a program needn't handle non-finite values.
Results may differ from the reference program's by a relative error of at most 0.017.
Values may be sent and summed in bfloat16 or wider, within the bound.
A program may use at most 192 MiB of HBM per device.

```python
import math
import jax
import jax.numpy as jnp
from jax import lax

HQ = 128
KEY_VALUE_HEADS = 8
HEAD_SIZE = 128
BLK = 64
QUERY_TOKENS = 256
QUERY_PER_KEY = 16
NBLK_DEV = 128
SEL_DEV = 16
MOST = 40
CONTEXT_TOKENS = 262144
CONTEXT_BLOCKS = 4096
SEL = 512


def draw_queries(key, part):
    inner = jax.random.fold_in(key, 101)
    base = jax.random.normal(inner, (QUERY_TOKENS, HQ, HEAD_SIZE), jnp.float32)
    drawn = jnp.clip(base, -48.0, 48.0)
    return drawn.astype(jnp.bfloat16)


def one_row(row_key):
    shards = CONTEXT_BLOCKS // NBLK_DEV
    first, second, third = jax.random.split(row_key, 3)
    order = jax.random.permutation(first, shards)
    rank = jnp.zeros((shards,), jnp.int32).at[order].set(jnp.arange(shards, dtype=jnp.int32))
    excess = MOST - SEL_DEV
    sizes = jax.random.randint(second, (shards,), 0, SEL_DEV // 2 + 1)
    paired = jnp.clip((rank - 3) // 2, 0, shards - 1)
    signed = jnp.where((rank - 3) % 2 == 0, 1, -1) * sizes[paired]
    alone = (rank == shards - 1) & ((shards - 3) % 2 == 1)
    delta = jnp.where(rank == 0, excess, jnp.where(rank == 1, -(excess // 2), jnp.where(rank == 2, -(excess - excess // 2), jnp.where(alone, 0, signed))))
    counts = SEL_DEV + delta
    perms = jax.vmap(lambda shard_key: jax.random.permutation(shard_key, NBLK_DEV))(jax.random.split(third, shards))
    chosen = (perms < counts[:, None]).reshape(-1)
    places = jnp.arange(CONTEXT_BLOCKS, dtype=jnp.int32)
    ordered = jnp.sort(jnp.where(chosen, places, CONTEXT_BLOCKS + places))
    return ordered[:SEL].astype(jnp.int32)


def draw_selection(key, part):
    keys_per_row = jax.random.split(jax.random.fold_in(key, 202), KEY_VALUE_HEADS)
    return jax.vmap(one_row)(keys_per_row)


def block_levels(own_key, dims, cuts, least, high):
    def one(axis_at, shards_of):
        steps = jax.random.uniform(jax.random.fold_in(jax.random.fold_in(own_key, 6), axis_at), (shards_of,), jnp.float32, least / len(cuts), high / len(cuts))
        return jnp.repeat(jnp.exp(steps), dims[axis_at] // shards_of).reshape((-1,) + (1,) * (len(dims) - axis_at - 1))

    loudness = one(*cuts[0])
    for cut in cuts[1:]:
        loudness = loudness * one(*cut)
    return loudness


def scatter_about(key, dims, deviation, limit, cuts=(), held_as=jnp.bfloat16):
    values = jax.random.normal(key, dims, jnp.float32) * deviation
    if len(cuts) > 0:
        values = block_levels(key, dims, cuts, -0.22, 0.18) * values
    return jnp.clip(values, min=-limit, max=limit).astype(held_as)


def setup_inputs(seed: int = 0) -> dict:
    key_of = jax.random.split(jax.random.key(seed), 7)
    queries = draw_queries(jax.random.fold_in(key_of[6], 71), 0)
    keys = scatter_about(key_of[1], (KEY_VALUE_HEADS, CONTEXT_TOKENS, HEAD_SIZE), 1.0, 6.0, ((0, 8), (1, 32)))
    values = scatter_about(key_of[2], (KEY_VALUE_HEADS, CONTEXT_TOKENS, HEAD_SIZE), 1.0, 6.0, ((0, 8), (1, 32)))
    key_block_scale = jnp.clip(jnp.exp(math.log(2.0) - 1.3862944 * jax.random.uniform(key_of[3], (KEY_VALUE_HEADS, CONTEXT_BLOCKS), jnp.float32) ** block_levels(key_of[3], (KEY_VALUE_HEADS, CONTEXT_BLOCKS), ((0, 8), (1, 32)), -0.2, 0.2)), 0.5, 2.0)
    value_block_scale = jnp.clip(jnp.exp(math.log(2.0) - 1.3862944 * jax.random.uniform(key_of[4], (KEY_VALUE_HEADS, CONTEXT_BLOCKS), jnp.float32) ** block_levels(key_of[4], (KEY_VALUE_HEADS, CONTEXT_BLOCKS), ((0, 8), (1, 32)), -0.2, 0.2)), 0.5, 2.0)
    selection = draw_selection(jax.random.fold_in(key_of[6], 71), 0)
    return {"queries": queries, "keys": keys, "values": values, "key_block_scale": key_block_scale, "value_block_scale": value_block_scale, "selection": selection}


def one_head(packed):
    query_group, key_head, value_head, key_scales, value_scales, chosen = packed
    key_rows = key_head.reshape(CONTEXT_BLOCKS, BLK, HEAD_SIZE)[chosen].reshape(SEL * BLK, HEAD_SIZE)
    value_rows = value_head.reshape(CONTEXT_BLOCKS, BLK, HEAD_SIZE)[chosen].reshape(SEL * BLK, HEAD_SIZE)
    key_factor = jnp.repeat(key_scales[chosen] * (1.0 / (HEAD_SIZE ** 0.5)), BLK, total_repeat_length=SEL * BLK)
    value_factor = jnp.repeat(value_scales[chosen], BLK, total_repeat_length=SEL * BLK)

    def one_query_head(query_rows):
        scores = jnp.dot(query_rows, key_rows.T, preferred_element_type=jnp.float32) * key_factor
        peak = jnp.max(scores, axis=1)
        prob = jnp.exp(scores - peak[:, None])
        total = jnp.sum(prob, axis=1)
        weights = (prob * value_factor).astype(jnp.bfloat16)
        summed = jnp.dot(weights, value_rows, preferred_element_type=jnp.float32)
        return summed / total[:, None]

    return lax.map(one_query_head, query_group)


def reference(queries, keys, values, key_block_scale, value_block_scale, selection):
    grouped_queries = queries.reshape(QUERY_TOKENS, KEY_VALUE_HEADS, QUERY_PER_KEY, HEAD_SIZE).transpose(1, 2, 0, 3)
    result = lax.map(one_head, (grouped_queries, keys, values, key_block_scale, value_block_scale, selection))
    return result.transpose(2, 0, 1, 3).reshape(QUERY_TOKENS, HQ, HEAD_SIZE).astype(jnp.bfloat16)
```

```python
import functools

import jax
import jax.numpy as jnp
from jax import lax
from jax.experimental import pallas as pl
from jax.experimental.pallas import tpu as pltpu
from jax.sharding import PartitionSpec as P

HEAD_SIZE = 128
BLK = 64
MOST = 40
GROUP = 16
KEYS = MOST * BLK
PART = 144
NZ, NX, NY = 8, 4, 4
NSTEP = 2 * NY
ROWS = 512
KC = 512
LOG2E = 1.4426950408889634
MESH = pl.DeviceIdType.MESH


def turn_of(step):
    u = step // 2
    return u + (u // 2) * (1 - 2 * (u % 2)), step % 2


def pack(acc, peak):
    total = acc[HEAD_SIZE : HEAD_SIZE + 1]
    high = total.astype(jnp.bfloat16).astype(jnp.float32)
    row = lax.broadcasted_iota(jnp.int32, (16, acc.shape[1]), 0)
    tail = jnp.where(row == 0, peak, jnp.where(row == 1, high, jnp.where(row == 2, total - high, 0.0)))
    return acc[:HEAD_SIZE].astype(jnp.bfloat16), tail.astype(jnp.bfloat16)


def merged(parts):
    tails = [part[HEAD_SIZE:PART, :].astype(jnp.float32) for part in parts]
    peak = functools.reduce(jnp.maximum, [tail[0:1] for tail in tails])
    total = jnp.zeros_like(peak)
    summed = jnp.zeros((HEAD_SIZE, 128), jnp.float32)
    for part, tail in zip(parts, tails):
        fade = jnp.exp2(tail[0:1] - peak)
        total = total + fade * (tail[1:2] + tail[2:3])
        summed = summed + fade * part[:HEAD_SIZE, :].astype(jnp.float32)
    return summed, total, peak


def kernel(
    q_hbm, k_hbm, v_hbm, ks_ref, vs_ref, sel_ref, selv_ref, out_ref,
    kbuf, vbuf, kk, vt, qbuf, xsend, xrecv, zsend, zrecv,
    local_sem, q_send, q_recv, x_send, x_recv, z_send, z_recv,
):
    ctx = lax.axis_index("ctx")
    head = lax.axis_index("head")
    z, x = ctx // NX, ctx % NX
    y, core = head // 2, head % 2
    local_blocks = kbuf.shape[0]

    def head_at(dy, dc):
        return ((y + dy) % NY) * 2 + (core + dc) % 2

    k_copy = pltpu.make_async_copy(k_hbm, kbuf, local_sem.at[0])
    v_copy = pltpu.make_async_copy(v_hbm, vbuf, local_sem.at[1])
    k_copy.start()
    v_copy.start()
    q_copy = pltpu.make_async_copy(
        q_hbm.at[:, pl.ds(pl.multiple_of(head * GROUP, GROUP), GROUP), :], qbuf.at[0], local_sem.at[2]
    )
    q_copy.start()

    barrier = pltpu.get_barrier_semaphore()
    for step in range(1, NSTEP):
        dy, dc = turn_of(step)
        pl.semaphore_signal(barrier, inc=1, device_id=(ctx, head_at(dy, dc)), device_id_type=MESH)
    for dx in range(1, NX):
        pl.semaphore_signal(barrier, inc=1, device_id=(z * NX + (x + dx) % NX, head), device_id_type=MESH)
    for dz in range(1, NZ):
        pl.semaphore_signal(barrier, inc=1, device_id=(((z + dz) % NZ) * NX + x, head), device_id_type=MESH)
    pl.semaphore_wait(barrier, NSTEP - 1 + NX - 1 + NZ - 1)

    def q_remote(step):
        dy, dc = turn_of(step)
        to = head_at(dy, dc)
        return pltpu.make_async_remote_copy(
            src_ref=q_hbm.at[:, pl.ds(pl.multiple_of(to * GROUP, GROUP), GROUP), :],
            dst_ref=qbuf.at[step],
            send_sem=q_send.at[step],
            recv_sem=q_recv.at[step],
            device_id=(ctx, to),
            device_id_type=MESH,
        )

    for step in range(1, NSTEP):
        q_remote(step).start()

    base = ctx * local_blocks
    chosen = selv_ref[...]
    first = jnp.sum((chosen < base).astype(jnp.int32))
    upto = jnp.sum((chosen < base + local_blocks).astype(jnp.int32))
    last = upto - 1
    factor = LOG2E / HEAD_SIZE**0.5

    k_copy.wait()
    v_copy.wait()

    def gather(pair, carry):
        value_parts = []
        mask_parts = []
        for half in range(2):
            j = first + pair * 2 + half
            place = jnp.maximum(jnp.minimum(j, last), 0)
            block = jnp.clip(sel_ref[0, place] - base, 0, local_blocks - 1)
            key_rows = kbuf[block].astype(jnp.float32) * (ks_ref[0, block] * factor)
            high = key_rows.astype(jnp.bfloat16)
            low = (key_rows - high.astype(jnp.float32)).astype(jnp.bfloat16)
            row = pl.multiple_of((pair * 2 + half) * BLK, BLK)
            kk[pl.ds(row, BLK), 0:HEAD_SIZE] = high
            kk[pl.ds(row, BLK), HEAD_SIZE : 2 * HEAD_SIZE] = low
            live = jnp.where(j <= last, 1.0, 0.0)
            value_parts.append(vbuf[block].astype(jnp.float32) * (vs_ref[0, block] * live))
            mask_parts.append(live)
        values = jnp.concatenate(value_parts, axis=0).T
        column = pl.ds(pl.multiple_of(pair * 2 * BLK, 2 * BLK), 2 * BLK)
        vt[0:HEAD_SIZE, column] = values.astype(jnp.bfloat16)
        lane = lax.broadcasted_iota(jnp.int32, (16, 2 * BLK), 1)
        vt[HEAD_SIZE:PART, column] = jnp.where(lane < BLK, mask_parts[0], mask_parts[1]).astype(jnp.bfloat16)
        return carry

    lax.fori_loop(0, MOST // 2, gather, 0)

    def attend(step):
        rows = qbuf[step].reshape(ROWS, HEAD_SIZE)
        turned = rows.T
        turned = jnp.concatenate([turned, turned], axis=0)
        peak = acc = None
        for i in range(KEYS // KC):
            scores = jnp.dot(kk[i * KC : (i + 1) * KC, :], turned, preferred_element_type=jnp.float32)
            best = jnp.max(scores, axis=0, keepdims=True)
            if i > 0:
                best = jnp.maximum(peak, best)
            best = best.astype(jnp.bfloat16).astype(jnp.float32)
            prob = jnp.exp2(scores - best).astype(jnp.bfloat16)
            added = jnp.dot(vt[:, i * KC : (i + 1) * KC], prob, preferred_element_type=jnp.float32)
            acc = added if i == 0 else acc * jnp.exp2(peak - best) + added
            peak = best
        summed, tail = pack(acc, peak)
        for part in range(NX):
            xsend[step, part, 0:HEAD_SIZE, :] = summed[:, part * 128 : (part + 1) * 128]
            xsend[step, part, HEAD_SIZE:PART, :] = tail[:, part * 128 : (part + 1) * 128]

    def x_remote(step, dx):
        to = (x + dx) % NX
        return pltpu.make_async_remote_copy(
            src_ref=xsend.at[step, to],
            dst_ref=xrecv.at[step, dx - 1],
            send_sem=x_send.at[step, dx - 1],
            recv_sem=x_recv.at[step, dx - 1],
            device_id=(z * NX + to, head),
            device_id_type=MESH,
        )

    def row_of(step):
        dy, dc = turn_of(step)
        return head_at(NY - dy, dc)

    def z_remote(step):
        to = row_of(step)
        slot = (z - to + NZ) % NZ - 1
        return pltpu.make_async_remote_copy(
            src_ref=zsend.at[step],
            dst_ref=zrecv.at[slot],
            send_sem=z_send.at[step],
            recv_sem=z_recv.at[slot],
            device_id=(to * NX + x, head),
            device_id_type=MESH,
        )

    def pass_on(step):
        for dx in range(1, NX):
            x_remote(step, dx).wait_recv()
        summed, total, peak = merged([xsend.at[step, x]] + [xrecv.at[step, dx] for dx in range(NX - 1)])
        acc = jnp.concatenate([summed, total], axis=0)
        summed, tail = pack(acc, peak)
        zsend[step, 0:HEAD_SIZE, :] = summed
        zsend[step, HEAD_SIZE:PART, :] = tail

        @pl.when(row_of(step) != z)
        def _():
            z_remote(step).start()

    q_copy.wait()

    def one_step(step, carry):
        @pl.when(step > 0)
        def _():
            q_remote(step).wait_recv()

        attend(step)
        for dx in range(1, NX):
            x_remote(step, dx).start()

        @pl.when(step > 0)
        def _():
            pass_on(step - 1)

        return carry

    lax.fori_loop(0, NSTEP, one_step, 0)
    pass_on(NSTEP - 1)

    own_y = (y - z // 2 + NY) % NY
    own_u = own_y + (own_y // 2) * (1 - 2 * (own_y % 2))
    own_step = own_u * 2 + (core + z) % 2
    for slot in range(NZ - 1):
        pltpu.make_async_remote_copy(
            src_ref=zsend.at[0],
            dst_ref=zrecv.at[slot],
            send_sem=z_send.at[0],
            recv_sem=z_recv.at[slot],
            device_id=(ctx, head),
            device_id_type=MESH,
        ).wait_recv()
    summed, total, _ = merged([zsend.at[own_step]] + [zrecv.at[slot] for slot in range(NZ - 1)])
    out_ref[...] = (summed / total).T.reshape(out_ref.shape).astype(out_ref.dtype)

    def finish(step, carry):
        for dx in range(1, NX):
            x_remote(step, dx).wait_send()

        @pl.when(step > 0)
        def _():
            q_remote(step).wait_send()

        @pl.when(row_of(step) != z)
        def _():
            z_remote(step).wait_send()

        return carry

    lax.fori_loop(0, NSTEP, finish, 0)


def on_device(queries, keys, values, key_block_scale, value_block_scale, selection):
    any_space = pl.BlockSpec(memory_space=pl.ANY)
    smem = pl.BlockSpec(memory_space=pltpu.SMEM)
    vmem = pl.BlockSpec(memory_space=pltpu.VMEM)
    tokens = queries.shape[0]
    blocks = (keys.shape[1] // BLK, BLK, HEAD_SIZE)
    dma = pltpu.SemaphoreType.DMA
    return pl.pallas_call(
        kernel,
        out_shape=jax.ShapeDtypeStruct((tokens // NX, GROUP, HEAD_SIZE), jnp.bfloat16),
        in_specs=[any_space] * 3 + [smem] * 3 + [vmem],
        out_specs=vmem,
        scratch_shapes=[
            pltpu.VMEM(blocks, jnp.bfloat16),
            pltpu.VMEM(blocks, jnp.bfloat16),
            pltpu.VMEM((KEYS, 2 * HEAD_SIZE), jnp.bfloat16),
            pltpu.VMEM((PART, KEYS), jnp.bfloat16),
            pltpu.VMEM((NSTEP, tokens, GROUP, HEAD_SIZE), jnp.bfloat16),
            pltpu.VMEM((NSTEP, NX, PART, 128), jnp.bfloat16),
            pltpu.VMEM((NSTEP, NX - 1, PART, 128), jnp.bfloat16),
            pltpu.VMEM((NSTEP, PART, 128), jnp.bfloat16),
            pltpu.VMEM((NZ - 1, PART, 128), jnp.bfloat16),
            dma((3,)),
            dma((NSTEP,)),
            dma((NSTEP,)),
            dma((NSTEP, NX - 1)),
            dma((NSTEP, NX - 1)),
            dma((NSTEP,)),
            dma((NZ - 1,)),
        ],
        compiler_params=pltpu.CompilerParams(
            collective_id=0, has_side_effects=True, vmem_limit_bytes=40 << 20
        ),
    )(queries, keys.reshape(blocks), values.reshape(blocks), key_block_scale, value_block_scale, selection, selection)


def solution(mesh):
    return jax.shard_map(
        on_device,
        mesh=mesh,
        in_specs=(
            P("head", None, None),
            P("head", "ctx", None),
            P("head", "ctx", None),
            P("head", "ctx"),
            P("head", "ctx"),
            P("head", None),
        ),
        out_specs=P("ctx", "head", None),
        check_vma=False,
    )
```

```python
import functools

import jax
import jax.numpy as jnp
from jax import lax
from jax.experimental import pallas as pl
from jax.experimental.pallas import tpu as pltpu
from jax.sharding import PartitionSpec as P

HEAD_SIZE = 128
BLK = 64
MOST = 40
GROUP = 16
KEYS = MOST * BLK
PART = 144
NZ, NX, NY = 8, 4, 4
NSTEP = 2 * NY
ROWS = 1024
KC = 512
TURNS = KEYS // KC
LOG2E = 1.4426950408889634
MESH = pl.DeviceIdType.MESH


def turn_of(step):
    u = step // 2
    return u + (u // 2) * (1 - 2 * (u % 2)), step % 2


def pack(acc, peak):
    total = acc[HEAD_SIZE : HEAD_SIZE + 1]
    high = total.astype(jnp.bfloat16).astype(jnp.float32)
    row = lax.broadcasted_iota(jnp.int32, (16, acc.shape[1]), 0)
    tail = jnp.where(row == 0, peak, jnp.where(row == 1, high, jnp.where(row == 2, total - high, 0.0)))
    return acc[:HEAD_SIZE].astype(jnp.bfloat16), tail.astype(jnp.bfloat16)


def merged(parts):
    tails = [part[HEAD_SIZE:PART, :].astype(jnp.float32) for part in parts]
    peak = functools.reduce(jnp.maximum, [tail[0:1] for tail in tails])
    total = jnp.zeros_like(peak)
    summed = jnp.zeros((HEAD_SIZE, 128), jnp.float32)
    for part, tail in zip(parts, tails):
        fade = jnp.exp2(tail[0:1] - peak)
        total = total + fade * (tail[1:2] + tail[2:3])
        summed = summed + fade * part[:HEAD_SIZE, :].astype(jnp.float32)
    return summed, total, peak


def kernel(
    q_hbm, k_hbm, v_hbm, ks_hbm, vs_hbm, sel_hbm, out_ref,
    kbuf, vbuf, kk, vt, qbuf, qt, held, xsend, xrecv, zsend, zrecv, ks_ref, vs_ref, sel_ref, selv_ref,
    local_sem, q_send, q_recv, x_send, x_recv, z_send, z_recv,
):
    ctx = lax.axis_index("ctx")
    head = lax.axis_index("head")
    z, x = ctx // NX, ctx % NX
    y, core = head // 2, head % 2
    local_blocks = kbuf.shape[0]

    def head_at(dy, dc):
        return ((y + dy) % NY) * 2 + (core + dc) % 2

    local = [
        pltpu.make_async_copy(sel_hbm, selv_ref, local_sem.at[0]),
        pltpu.make_async_copy(sel_hbm, sel_ref, local_sem.at[1]),
        pltpu.make_async_copy(ks_hbm, ks_ref, local_sem.at[2]),
        pltpu.make_async_copy(vs_hbm, vs_ref, local_sem.at[3]),
        pltpu.make_async_copy(
            q_hbm.at[:, pl.ds(pl.multiple_of(head * GROUP, GROUP), GROUP), :], qbuf.at[0], local_sem.at[4]
        ),
    ]
    half = local_blocks // 2
    for k in range(2):
        part = pl.ds(k * half, half)
        local.append(pltpu.make_async_copy(k_hbm.at[part], kbuf.at[part], local_sem.at[5 + k]))
    for k in range(2):
        part = pl.ds(k * half, half)
        local.append(pltpu.make_async_copy(v_hbm.at[part], vbuf.at[part], local_sem.at[7 + k]))
    for copy in local:
        copy.start()

    barrier = pltpu.get_barrier_semaphore()
    for step in range(1, NSTEP):
        dy, dc = turn_of(step)
        pl.semaphore_signal(barrier, inc=1, device_id=(ctx, head_at(dy, dc)), device_id_type=MESH)
    for dx in range(1, NX):
        pl.semaphore_signal(barrier, inc=1, device_id=(z * NX + (x + dx) % NX, head), device_id_type=MESH)
    for dz in range(1, NZ):
        pl.semaphore_signal(barrier, inc=1, device_id=(((z + dz) % NZ) * NX + x, head), device_id_type=MESH)
    pl.semaphore_wait(barrier, NSTEP - 1 + NX - 1 + NZ - 1)

    def q_remote(step):
        dy, dc = turn_of(step)
        to = head_at(dy, dc)
        return pltpu.make_async_remote_copy(
            src_ref=q_hbm.at[:, pl.ds(pl.multiple_of(to * GROUP, GROUP), GROUP), :],
            dst_ref=qbuf.at[step],
            send_sem=q_send.at[step],
            recv_sem=q_recv.at[step],
            device_id=(ctx, to),
            device_id_type=MESH,
        )

    for step in range(1, NSTEP):
        q_remote(step).start()

    for copy in local[:4]:
        copy.wait()
    base = ctx * local_blocks
    chosen = selv_ref[...]
    first = jnp.sum((chosen < base).astype(jnp.int32))
    last = jnp.sum((chosen < base + local_blocks).astype(jnp.int32)) - 1
    factor = LOG2E / HEAD_SIZE**0.5

    for copy in local[5:]:
        copy.wait()

    def gather(turn):
        for pair in range(turn * KC // (2 * BLK), (turn + 1) * KC // (2 * BLK)):
            value_parts = []
            mask_parts = []
            for side in range(2):
                j = first + pair * 2 + side
                place = jnp.maximum(jnp.minimum(j, last), 0)
                block = jnp.clip(sel_ref[0, place] - base, 0, local_blocks - 1)
                key_rows = kbuf[block].astype(jnp.float32) * (ks_ref[0, block] * factor)
                high = key_rows.astype(jnp.bfloat16)
                low = (key_rows - high.astype(jnp.float32)).astype(jnp.bfloat16)
                row = (pair * 2 + side) * BLK
                kk[row : row + BLK, 0:HEAD_SIZE] = high
                kk[row : row + BLK, HEAD_SIZE : 2 * HEAD_SIZE] = low
                live = jnp.where(j <= last, 1.0, 0.0)
                value_parts.append(vbuf[block].astype(jnp.float32) * (vs_ref[0, block] * live))
                mask_parts.append(live)
            values = jnp.concatenate(value_parts, axis=0).astype(jnp.bfloat16).T
            column = pl.ds(pair * 2 * BLK, 2 * BLK)
            vt[0:HEAD_SIZE, column] = values
            lane = lax.broadcasted_iota(jnp.int32, (16, 2 * BLK), 1)
            vt[HEAD_SIZE:PART, column] = jnp.where(lane < BLK, mask_parts[0], mask_parts[1]).astype(jnp.bfloat16)

    def turned(step):
        rows = qbuf[pl.ds(step * 2, 2)].reshape(ROWS, HEAD_SIZE)
        flat = rows.T
        return jnp.concatenate([flat, flat], axis=0)

    def scores_of(turn, queries):
        return jnp.dot(kk[turn * KC : (turn + 1) * KC, :], queries, preferred_element_type=jnp.float32)

    def x_remote(step, dx):
        to = (x + dx) % NX
        return pltpu.make_async_remote_copy(
            src_ref=xsend.at[step, to],
            dst_ref=xrecv.at[step, dx - 1],
            send_sem=x_send.at[step, dx - 1],
            recv_sem=x_recv.at[step, dx - 1],
            device_id=(z * NX + to, head),
            device_id_type=MESH,
        )

    def row_of(chunk):
        dy, dc = turn_of(chunk)
        return head_at(NY - dy, dc)

    def z_remote(chunk):
        to = row_of(chunk)
        slot = (z - to + NZ) % NZ - 1
        return pltpu.make_async_remote_copy(
            src_ref=zsend.at[chunk],
            dst_ref=zrecv.at[slot],
            send_sem=z_send.at[chunk],
            recv_sem=z_recv.at[slot],
            device_id=(to * NX + x, head),
            device_id_type=MESH,
        )

    def pass_on(step):
        for dx in range(1, NX):
            x_remote(step, dx).wait_recv()
        for side in range(2):
            chunk = step * 2 + side
            summed, total, peak = merged(
                [xsend.at[step, x, side]] + [xrecv.at[step, dx, side] for dx in range(NX - 1)]
            )
            summed, tail = pack(jnp.concatenate([summed, total], axis=0), peak)
            zsend[chunk, 0:HEAD_SIZE, :] = summed
            zsend[chunk, HEAD_SIZE:PART, :] = tail

            @pl.when(row_of(chunk) != z)
            def _():
                z_remote(chunk).start()

    def one_step(step, first_step, last_step):
        queries = qt[step % 2]
        scores = held[...]
        peak = acc = None
        for i in range(TURNS):
            if i < TURNS - 1:
                if first_step:
                    gather(i + 1)
                coming = scores_of(i + 1, queries)
            elif not last_step:
                for side in range(2):
                    q_remote(step * 2 + 2 + side).wait_recv()
                following = turned(step + 1)
                qt[(step + 1) % 2] = following
                held[...] = scores_of(0, following)
            best = jnp.max(scores, axis=0, keepdims=True)
            if i > 0:
                best = jnp.maximum(peak, best)
            best = best.astype(jnp.bfloat16).astype(jnp.float32)
            prob = jnp.exp2(scores - best).astype(jnp.bfloat16)
            added = jnp.dot(vt[:, i * KC : (i + 1) * KC], prob, preferred_element_type=jnp.float32)
            acc = added if i == 0 else acc * jnp.exp2(peak - best) + added
            peak = best
            scores = coming
            if i == 2 and not first_step:
                pass_on(step - 1)
        summed, tail = pack(acc, peak)
        for side in range(2):
            for part in range(NX):
                lanes = slice((side * NX + part) * 128, (side * NX + part + 1) * 128)
                xsend[step, part, side, 0:HEAD_SIZE, :] = summed[:, lanes]
                xsend[step, part, side, HEAD_SIZE:PART, :] = tail[:, lanes]
        for dx in range(1, NX):
            x_remote(step, dx).start()

    gather(0)
    local[4].wait()
    q_remote(1).wait_recv()
    queries = turned(0)
    qt[0] = queries
    held[...] = scores_of(0, queries)
    one_step(0, True, False)

    def middle(step, carry):
        one_step(step, False, False)
        return carry

    lax.fori_loop(1, NY - 1, middle, 0)
    one_step(NY - 1, False, True)
    pass_on(NY - 1)

    own_y = (y - z // 2 + NY) % NY
    own_u = own_y + (own_y // 2) * (1 - 2 * (own_y % 2))
    own_chunk = own_u * 2 + (core + z) % 2
    for slot in range(NZ - 1):
        pltpu.make_async_remote_copy(
            src_ref=zsend.at[0],
            dst_ref=zrecv.at[slot],
            send_sem=z_send.at[0],
            recv_sem=z_recv.at[slot],
            device_id=(ctx, head),
            device_id_type=MESH,
        ).wait_recv()
    summed, total, _ = merged([zsend.at[own_chunk]] + [zrecv.at[slot] for slot in range(NZ - 1)])
    out_ref[...] = (summed / total).T.reshape(out_ref.shape).astype(out_ref.dtype)

    def finish(chunk, carry):
        @pl.when(chunk < NY)
        def _():
            for dx in range(1, NX):
                x_remote(chunk, dx).wait_send()

        @pl.when(chunk > 0)
        def _():
            q_remote(chunk).wait_send()

        @pl.when(row_of(chunk) != z)
        def _():
            z_remote(chunk).wait_send()

        return carry

    lax.fori_loop(0, NSTEP, finish, 0)


def on_device(queries, keys, values, key_block_scale, value_block_scale, selection):
    hbm = pl.BlockSpec(memory_space=pltpu.HBM)
    tokens = queries.shape[0]
    blocks = (keys.shape[1] // BLK, BLK, HEAD_SIZE)
    dma = pltpu.SemaphoreType.DMA
    return pl.pallas_call(
        kernel,
        out_shape=jax.ShapeDtypeStruct((tokens // NX, GROUP, HEAD_SIZE), jnp.bfloat16),
        in_specs=[hbm] * 6,
        out_specs=pl.BlockSpec(memory_space=pltpu.VMEM),
        scratch_shapes=[
            pltpu.VMEM(blocks, jnp.bfloat16),
            pltpu.VMEM(blocks, jnp.bfloat16),
            pltpu.VMEM((KEYS, 2 * HEAD_SIZE), jnp.bfloat16),
            pltpu.VMEM((PART, KEYS), jnp.bfloat16),
            pltpu.VMEM((NSTEP, tokens, GROUP, HEAD_SIZE), jnp.bfloat16),
            pltpu.VMEM((2, 2 * HEAD_SIZE, ROWS), jnp.bfloat16),
            pltpu.VMEM((KC, ROWS), jnp.float32),
            pltpu.VMEM((NY, NX, 2, PART, 128), jnp.bfloat16),
            pltpu.VMEM((NY, NX - 1, 2, PART, 128), jnp.bfloat16),
            pltpu.VMEM((NSTEP, PART, 128), jnp.bfloat16),
            pltpu.VMEM((NZ - 1, PART, 128), jnp.bfloat16),
            pltpu.SMEM((1, keys.shape[1] // BLK), jnp.float32),
            pltpu.SMEM((1, keys.shape[1] // BLK), jnp.float32),
            pltpu.SMEM(selection.shape, jnp.int32),
            pltpu.VMEM(selection.shape, jnp.int32),
            dma((9,)),
            dma((NSTEP,)),
            dma((NSTEP,)),
            dma((NY, NX - 1)),
            dma((NY, NX - 1)),
            dma((NSTEP,)),
            dma((NZ - 1,)),
        ],
        compiler_params=pltpu.CompilerParams(
            collective_id=0, has_side_effects=True, vmem_limit_bytes=60 << 20
        ),
    )(queries, keys.reshape(blocks), values.reshape(blocks), key_block_scale, value_block_scale, selection)


def solution(mesh):
    return jax.shard_map(
        on_device,
        mesh=mesh,
        in_specs=(
            P("head", None, None),
            P("head", "ctx", None),
            P("head", "ctx", None),
            P("head", "ctx"),
            P("head", "ctx"),
            P("head", None),
        ),
        out_specs=P("ctx", "head", None),
        check_vma=False,
    )
```

```python
import functools

import jax
import jax.numpy as jnp
from jax import lax
from jax.experimental import pallas as pl
from jax.experimental.pallas import tpu as pltpu
from jax.sharding import PartitionSpec as P

HEAD_SIZE = 128
BLK = 64
MOST = 40
GROUP = 16
KEYS = MOST * BLK
PART = 144
NZ, NX, NY = 8, 4, 4
NSTEP = 2 * NY
ROWS = 512
FIRST_KC, KC = 512, 1280
LOG2E = 1.4426950408889634
MESH = pl.DeviceIdType.MESH


def turn_of(step):
    far, k = (step + 6) // 8, (step + 4) % 6
    return far * (1 + 2 * (k % 3 % 2) + k % 3 // 2), far * (k // 3) + (1 - far) * step


def step_of(dy, dc):
    far = (dy + 3) // 4
    return dc + far * (2 + 2 * dc + (dy // 2) * (4 - dy))


def pack(acc, peak):
    total = acc[HEAD_SIZE : HEAD_SIZE + 1]
    high = total.astype(jnp.bfloat16).astype(jnp.float32)
    row = lax.broadcasted_iota(jnp.int32, (16, acc.shape[1]), 0)
    tail = jnp.where(row == 0, peak, jnp.where(row == 1, high, jnp.where(row == 2, total - high, 0.0)))
    return acc[:HEAD_SIZE].astype(jnp.bfloat16), tail.astype(jnp.bfloat16)


def merged(parts):
    tails = [part[HEAD_SIZE:PART, :].astype(jnp.float32) for part in parts]
    peak = functools.reduce(jnp.maximum, [tail[0:1] for tail in tails])
    total = jnp.zeros_like(peak)
    summed = jnp.zeros((HEAD_SIZE, 128), jnp.float32)
    for part, tail in zip(parts, tails):
        fade = jnp.exp2(tail[0:1] - peak)
        total = total + fade * (tail[1:2] + tail[2:3])
        summed = summed + fade * part[:HEAD_SIZE, :].astype(jnp.float32)
    return summed, total, peak


def kernel(
    q_hbm, k_hbm, v_hbm, ks_hbm, vs_hbm, sel_hbm, out_ref,
    kbuf, vbuf, kk, vt, qbuf, qt, held, xsend, xrecv, zsend, zrecv, ks_ref, vs_ref, sel_ref, selv_ref,
    local_sem, q_send, q_recv, x_send, x_recv, z_send, z_recv,
):
    ctx = lax.axis_index("ctx")
    head = lax.axis_index("head")
    z, x = ctx // NX, ctx % NX
    y, core = head // 2, head % 2
    local_blocks = kbuf.shape[0]

    def head_at(dy, dc):
        return ((y + dy) % NY) * 2 + (core + dc) % 2

    local = [
        pltpu.make_async_copy(sel_hbm, selv_ref, local_sem.at[0]),
        pltpu.make_async_copy(sel_hbm, sel_ref, local_sem.at[1]),
        pltpu.make_async_copy(ks_hbm, ks_ref, local_sem.at[2]),
        pltpu.make_async_copy(vs_hbm, vs_ref, local_sem.at[3]),
        pltpu.make_async_copy(
            q_hbm.at[:, pl.ds(pl.multiple_of(head * GROUP, GROUP), GROUP), :], qbuf.at[0], local_sem.at[4]
        ),
    ]
    half = local_blocks // 2
    for k in range(2):
        part = pl.ds(k * half, half)
        local.append(pltpu.make_async_copy(k_hbm.at[part], kbuf.at[part], local_sem.at[5 + k]))
    for k in range(2):
        part = pl.ds(k * half, half)
        local.append(pltpu.make_async_copy(v_hbm.at[part], vbuf.at[part], local_sem.at[7 + k]))
    for copy in local:
        copy.start()

    barrier = pltpu.get_barrier_semaphore()
    for step in range(1, NSTEP):
        dy, dc = turn_of(step)
        pl.semaphore_signal(barrier, inc=1, device_id=(ctx, head_at(dy, dc)), device_id_type=MESH)
    for dx in range(1, NX):
        pl.semaphore_signal(barrier, inc=1, device_id=(z * NX + (x + dx) % NX, head), device_id_type=MESH)
    for dz in range(1, NZ):
        pl.semaphore_signal(barrier, inc=1, device_id=(((z + dz) % NZ) * NX + x, head), device_id_type=MESH)
    pl.semaphore_wait(barrier, NSTEP - 1 + NX - 1 + NZ - 1)

    def q_remote(step):
        dy, dc = turn_of(step)
        to = head_at(dy, dc)
        return pltpu.make_async_remote_copy(
            src_ref=q_hbm.at[:, pl.ds(pl.multiple_of(to * GROUP, GROUP), GROUP), :],
            dst_ref=qbuf.at[step],
            send_sem=q_send.at[step],
            recv_sem=q_recv.at[step],
            device_id=(ctx, to),
            device_id_type=MESH,
        )

    for step in range(1, 4):
        q_remote(step).start()

    for copy in local[:4]:
        copy.wait()
    base = ctx * local_blocks
    chosen = selv_ref[...]
    first = jnp.sum((chosen < base).astype(jnp.int32))
    last = jnp.sum((chosen < base + local_blocks).astype(jnp.int32)) - 1
    factor = LOG2E / HEAD_SIZE**0.5

    for copy in local[5:]:
        copy.wait()

    def gather(turn):
        for pair in range(turn * FIRST_KC // (2 * BLK), (turn + 1) * FIRST_KC // (2 * BLK)):
            value_parts = []
            mask_parts = []
            for side in range(2):
                j = first + pair * 2 + side
                place = jnp.maximum(jnp.minimum(j, last), 0)
                block = jnp.clip(sel_ref[0, place] - base, 0, local_blocks - 1)
                key_rows = kbuf[block].astype(jnp.float32) * (ks_ref[0, block] * factor)
                high = key_rows.astype(jnp.bfloat16)
                low = (key_rows - high.astype(jnp.float32)).astype(jnp.bfloat16)
                row = (pair * 2 + side) * BLK
                kk[row : row + BLK, 0:HEAD_SIZE] = high
                kk[row : row + BLK, HEAD_SIZE : 2 * HEAD_SIZE] = low
                live = jnp.where(j <= last, 1.0, 0.0)
                value_parts.append(vbuf[block].astype(jnp.float32) * (vs_ref[0, block] * live))
                mask_parts.append(live)
            values = jnp.concatenate(value_parts, axis=0).astype(jnp.bfloat16).T
            column = pl.ds(pair * 2 * BLK, 2 * BLK)
            vt[0:HEAD_SIZE, column] = values
            lane = lax.broadcasted_iota(jnp.int32, (16, 2 * BLK), 1)
            vt[HEAD_SIZE:PART, column] = jnp.where(lane < BLK, mask_parts[0], mask_parts[1]).astype(jnp.bfloat16)

    def turned(step):
        flat = qbuf[step].reshape(ROWS, HEAD_SIZE).T
        return jnp.concatenate([flat, flat], axis=0)

    def scores_of(start, keys, queries):
        return jnp.dot(kk[start : start + keys, :], queries, preferred_element_type=jnp.float32)

    def x_remote(step, dx):
        to = (x + dx) % NX
        return pltpu.make_async_remote_copy(
            src_ref=xsend.at[step, to],
            dst_ref=xrecv.at[step, dx - 1],
            send_sem=x_send.at[step, dx - 1],
            recv_sem=x_recv.at[step, dx - 1],
            device_id=(z * NX + to, head),
            device_id_type=MESH,
        )

    def row_of(step):
        dy, dc = turn_of(step)
        return head_at(NY - dy, dc)

    def z_remote(step):
        to = row_of(step)
        slot = (z - to + NZ) % NZ - 1
        return pltpu.make_async_remote_copy(
            src_ref=zsend.at[step],
            dst_ref=zrecv.at[slot],
            send_sem=z_send.at[step],
            recv_sem=z_recv.at[slot],
            device_id=(to * NX + x, head),
            device_id_type=MESH,
        )

    def pass_on(step):
        for dx in range(1, NX):
            x_remote(step, dx).wait_recv()
        summed, total, peak = merged([xsend.at[step, x]] + [xrecv.at[step, dx] for dx in range(NX - 1)])
        summed, tail = pack(jnp.concatenate([summed, total], axis=0), peak)
        zsend[step, 0:HEAD_SIZE, :] = summed
        zsend[step, HEAD_SIZE:PART, :] = tail

        @pl.when(row_of(step) != z)
        def _():
            z_remote(step).start()

    def one_step(step, first_step, last_step):
        keys = FIRST_KC if first_step else KC
        queries = qt[step % 2]
        if first_step:
            gather(0)
            scores = scores_of(0, keys, queries)
        else:
            scores = held[...]
        peak = acc = None
        for start in range(0, KEYS, keys):
            if start + keys < KEYS:
                if first_step:
                    gather(start // keys + 1)
                coming = scores_of(start + keys, keys, queries)
            elif not last_step:
                q_remote(step + 1).wait_recv()
                following = turned(step + 1)
                qt[(step + 1) % 2] = following
                held[...] = scores_of(0, KC, following)
            best = jnp.max(scores, axis=0, keepdims=True)
            if start > 0:
                best = jnp.maximum(peak, best)
            best = best.astype(jnp.bfloat16).astype(jnp.float32)
            prob = jnp.exp2(scores - best).astype(jnp.bfloat16)
            added = jnp.dot(vt[:, start : start + keys], prob, preferred_element_type=jnp.float32)
            acc = added if start == 0 else acc * jnp.exp2(peak - best) + added
            peak = best
            scores = coming
        summed, tail = pack(acc, peak)
        for part in range(NX):
            xsend[step, part, 0:HEAD_SIZE, :] = summed[:, part * 128 : (part + 1) * 128]
            xsend[step, part, HEAD_SIZE:PART, :] = tail[:, part * 128 : (part + 1) * 128]
        for dx in range(1, NX):
            x_remote(step, dx).start()

    local[4].wait()
    qt[0] = turned(0)
    q_remote(4).start()
    one_step(0, True, False)

    def middle(step, carry):
        @pl.when(step < 4)
        def _():
            q_remote(step + 4).start()

        one_step(step, False, False)

        @pl.when(step > 1)
        def _():
            pass_on(step - 2)

        return carry

    lax.fori_loop(1, NSTEP - 1, middle, 0)
    one_step(NSTEP - 1, False, True)
    for step in range(NSTEP - 3, NSTEP):
        pass_on(step)

    own_y = (y - z // 2 + NY) % NY
    own_step = step_of(own_y, (core + z) % 2)
    for slot in range(NZ - 1):
        pltpu.make_async_remote_copy(
            src_ref=zsend.at[0],
            dst_ref=zrecv.at[slot],
            send_sem=z_send.at[0],
            recv_sem=z_recv.at[slot],
            device_id=(ctx, head),
            device_id_type=MESH,
        ).wait_recv()
    summed, total, _ = merged([zsend.at[own_step]] + [zrecv.at[slot] for slot in range(NZ - 1)])
    out_ref[...] = (summed / total).T.reshape(out_ref.shape).astype(out_ref.dtype)

    def finish(step, carry):
        for dx in range(1, NX):
            x_remote(step, dx).wait_send()

        @pl.when(step > 0)
        def _():
            q_remote(step).wait_send()

        @pl.when(row_of(step) != z)
        def _():
            z_remote(step).wait_send()

        return carry

    lax.fori_loop(0, NSTEP, finish, 0)


def on_device(queries, keys, values, key_block_scale, value_block_scale, selection):
    hbm = pl.BlockSpec(memory_space=pltpu.HBM)
    tokens = queries.shape[0]
    blocks = (keys.shape[1] // BLK, BLK, HEAD_SIZE)
    dma = pltpu.SemaphoreType.DMA
    return pl.pallas_call(
        kernel,
        out_shape=jax.ShapeDtypeStruct((tokens // NX, GROUP, HEAD_SIZE), jnp.bfloat16),
        in_specs=[hbm] * 6,
        out_specs=pl.BlockSpec(memory_space=pltpu.VMEM),
        scratch_shapes=[
            pltpu.VMEM(blocks, jnp.bfloat16),
            pltpu.VMEM(blocks, jnp.bfloat16),
            pltpu.VMEM((KEYS, 2 * HEAD_SIZE), jnp.bfloat16),
            pltpu.VMEM((PART, KEYS), jnp.bfloat16),
            pltpu.VMEM((NSTEP, tokens, GROUP, HEAD_SIZE), jnp.bfloat16),
            pltpu.VMEM((2, 2 * HEAD_SIZE, ROWS), jnp.bfloat16),
            pltpu.VMEM((KC, ROWS), jnp.float32),
            pltpu.VMEM((NSTEP, NX, PART, 128), jnp.bfloat16),
            pltpu.VMEM((NSTEP, NX - 1, PART, 128), jnp.bfloat16),
            pltpu.VMEM((NSTEP, PART, 128), jnp.bfloat16),
            pltpu.VMEM((NZ - 1, PART, 128), jnp.bfloat16),
            pltpu.SMEM((1, keys.shape[1] // BLK), jnp.float32),
            pltpu.SMEM((1, keys.shape[1] // BLK), jnp.float32),
            pltpu.SMEM(selection.shape, jnp.int32),
            pltpu.VMEM(selection.shape, jnp.int32),
            dma((9,)),
            dma((NSTEP,)),
            dma((NSTEP,)),
            dma((NSTEP, NX - 1)),
            dma((NSTEP, NX - 1)),
            dma((NSTEP,)),
            dma((NZ - 1,)),
        ],
        compiler_params=pltpu.CompilerParams(
            collective_id=0, has_side_effects=True, vmem_limit_bytes=60 << 20
        ),
    )(queries, keys.reshape(blocks), values.reshape(blocks), key_block_scale, value_block_scale, selection)


def solution(mesh):
    return jax.shard_map(
        on_device,
        mesh=mesh,
        in_specs=(
            P("head", None, None),
            P("head", "ctx", None),
            P("head", "ctx", None),
            P("head", "ctx"),
            P("head", "ctx"),
            P("head", None),
        ),
        out_specs=P("ctx", "head", None),
        check_vma=False,
    )
```

```python
import functools

import jax
import jax.numpy as jnp
from jax import lax
from jax.experimental import pallas as pl
from jax.experimental.pallas import tpu as pltpu
from jax.sharding import PartitionSpec as P

HEAD_SIZE = 128
BLK = 64
MOST = 40
GROUP = 16
KEYS = MOST * BLK
PART = 144
NZ, NX, NY = 8, 4, 4
NSTEP = 2 * NY
ROWS = 512
FIRST_KC, KC = 512, 1280
LOG2E = 1.4426950408889634
MESH = pl.DeviceIdType.MESH


def turn_of(step):
    far, k = (step + 6) // 8, (step + 4) % 6
    return far * (1 + 2 * (k % 3 % 2) + k % 3 // 2), far * (k // 3) + (1 - far) * step


def step_of(dy, dc):
    far = (dy + 3) // 4
    return dc + far * (2 + 2 * dc + (dy // 2) * (4 - dy))


def pack(acc, peak):
    total = acc[HEAD_SIZE : HEAD_SIZE + 1]
    high = total.astype(jnp.bfloat16).astype(jnp.float32)
    row = lax.broadcasted_iota(jnp.int32, (16, acc.shape[1]), 0)
    tail = jnp.where(row == 0, peak, jnp.where(row == 1, high, jnp.where(row == 2, total - high, 0.0)))
    return acc[:HEAD_SIZE].astype(jnp.bfloat16), tail.astype(jnp.bfloat16)


def merged(parts):
    tails = [part[HEAD_SIZE:PART, :].astype(jnp.float32) for part in parts]
    peak = functools.reduce(jnp.maximum, [tail[0:1] for tail in tails])
    total = jnp.zeros_like(peak)
    summed = jnp.zeros((HEAD_SIZE, 128), jnp.float32)
    for part, tail in zip(parts, tails):
        fade = jnp.exp2(tail[0:1] - peak)
        total = total + fade * (tail[1:2] + tail[2:3])
        summed = summed + fade * part[:HEAD_SIZE, :].astype(jnp.float32)
    return summed, total, peak


def kernel(
    q_hbm, k_hbm, v_hbm, ks_hbm, vs_hbm, sel_hbm, out_ref,
    kbuf, vbuf, kk, vt, qbuf, qt, held, xsend, xrecv, zsend, zrecv, ks_ref, vs_ref, sel_ref, selv_ref,
    local_sem, q_send, q_recv, x_send, x_recv, z_send, z_recv,
):
    ctx = lax.axis_index("ctx")
    head = lax.axis_index("head")
    z, x = ctx // NX, ctx % NX
    y, core = head // 2, head % 2
    local_blocks = kbuf.shape[0]
    share = q_hbm.shape[0] // 4

    def head_at(dy, dc):
        return ((y + dy) % NY) * 2 + (core + dc) % 2

    local = [
        pltpu.make_async_copy(sel_hbm, selv_ref, local_sem.at[0]),
        pltpu.make_async_copy(sel_hbm, sel_ref, local_sem.at[1]),
        pltpu.make_async_copy(ks_hbm, ks_ref, local_sem.at[2]),
        pltpu.make_async_copy(vs_hbm, vs_ref, local_sem.at[3]),
        pltpu.make_async_copy(
            q_hbm.at[:, pl.ds(pl.multiple_of(head * GROUP, GROUP), GROUP), :], qbuf.at[0], local_sem.at[4]
        ),
    ]
    half = local_blocks // 2
    for k in range(2):
        part = pl.ds(k * half, half)
        local.append(pltpu.make_async_copy(k_hbm.at[part], kbuf.at[part], local_sem.at[5 + k]))
    for k in range(2):
        part = pl.ds(k * half, half)
        local.append(pltpu.make_async_copy(v_hbm.at[part], vbuf.at[part], local_sem.at[7 + k]))
    for copy in local:
        copy.start()

    barrier = pltpu.get_barrier_semaphore()
    for step in range(1, NSTEP):
        dy, dc = turn_of(step)
        pl.semaphore_signal(barrier, inc=1, device_id=(ctx, head_at(dy, dc)), device_id_type=MESH)
    for dx in range(1, NX):
        pl.semaphore_signal(barrier, inc=1, device_id=(z * NX + (x + dx) % NX, head), device_id_type=MESH)
    for dz in range(1, NZ):
        pl.semaphore_signal(barrier, inc=1, device_id=(((z + dz) % NZ) * NX + x, head), device_id_type=MESH)
    pl.semaphore_wait(barrier, NSTEP - 1 + NX - 1 + NZ - 1)

    def label_at(turn):
        return turn + turn // 6 * core * (13 - 2 * turn)

    def q_mate():
        to = head_at(0, 1)
        return pltpu.make_async_remote_copy(
            src_ref=q_hbm.at[:, pl.ds(pl.multiple_of(to * GROUP, GROUP), GROUP), :],
            dst_ref=qbuf.at[1],
            send_sem=q_send.at[0, 0],
            recv_sem=q_recv.at[0, 0],
            device_id=(ctx, to),
            device_id_type=MESH,
        )

    def quarter(k):
        return pl.ds((z + k) % 4 * share, share)

    def q_direct(step, k):
        dy, dc = turn_of(step)
        to = head_at(dy, dc)
        return pltpu.make_async_remote_copy(
            src_ref=q_hbm.at[quarter(k), pl.ds(pl.multiple_of(to * GROUP, GROUP), GROUP), :],
            dst_ref=qbuf.at[step, quarter(k)],
            send_sem=q_send.at[step, k],
            recv_sem=q_recv.at[step, k],
            device_id=(ctx, to),
            device_id_type=MESH,
        )

    def q_relay(step, k):
        to = (z + 1 + k * (NZ - 2)) % NZ
        return pltpu.make_async_remote_copy(
            src_ref=qbuf.at[step, quarter(k)],
            dst_ref=qbuf.at[step, quarter(k)],
            send_sem=q_send.at[step, 2 + k],
            recv_sem=q_recv.at[step, 2 + k],
            device_id=(to * NX + x, head),
            device_id_type=MESH,
        )

    def fetch(step):
        for k in range(2):
            q_direct(step, k).start()

    def forward(step):
        for k in range(2):
            q_direct(step, k).wait_recv()
            q_relay(step, k).start()

    q_mate().start()
    fetch(2)
    fetch(3)

    for copy in local[:4]:
        copy.wait()
    base = ctx * local_blocks
    chosen = selv_ref[...]
    first = jnp.sum((chosen < base).astype(jnp.int32))
    last = jnp.sum((chosen < base + local_blocks).astype(jnp.int32)) - 1
    factor = LOG2E / HEAD_SIZE**0.5

    for copy in local[5:]:
        copy.wait()

    def gather(turn):
        for pair in range(turn * FIRST_KC // (2 * BLK), (turn + 1) * FIRST_KC // (2 * BLK)):
            value_parts = []
            mask_parts = []
            for side in range(2):
                j = first + pair * 2 + side
                place = jnp.maximum(jnp.minimum(j, last), 0)
                block = jnp.clip(sel_ref[0, place] - base, 0, local_blocks - 1)
                key_rows = kbuf[block].astype(jnp.float32) * (ks_ref[0, block] * factor)
                high = key_rows.astype(jnp.bfloat16)
                low = (key_rows - high.astype(jnp.float32)).astype(jnp.bfloat16)
                row = (pair * 2 + side) * BLK
                kk[row : row + BLK, 0:HEAD_SIZE] = high
                kk[row : row + BLK, HEAD_SIZE : 2 * HEAD_SIZE] = low
                live = jnp.where(j <= last, 1.0, 0.0)
                value_parts.append(vbuf[block].astype(jnp.float32) * (vs_ref[0, block] * live))
                mask_parts.append(live)
            values = jnp.concatenate(value_parts, axis=0).astype(jnp.bfloat16).T
            column = pl.ds(pair * 2 * BLK, 2 * BLK)
            vt[0:HEAD_SIZE, column] = values
            lane = lax.broadcasted_iota(jnp.int32, (16, 2 * BLK), 1)
            vt[HEAD_SIZE:PART, column] = jnp.where(lane < BLK, mask_parts[0], mask_parts[1]).astype(jnp.bfloat16)

    def turned(step):
        flat = qbuf[step].reshape(ROWS, HEAD_SIZE).T
        return jnp.concatenate([flat, flat], axis=0)

    def scores_of(start, keys, queries):
        return jnp.dot(kk[start : start + keys, :], queries, preferred_element_type=jnp.float32)

    def x_remote(step, dx):
        to = (x + dx) % NX
        return pltpu.make_async_remote_copy(
            src_ref=xsend.at[step, to],
            dst_ref=xrecv.at[step, dx - 1],
            send_sem=x_send.at[step, dx - 1],
            recv_sem=x_recv.at[step, dx - 1],
            device_id=(z * NX + to, head),
            device_id_type=MESH,
        )

    def row_of(step):
        dy, dc = turn_of(step)
        return head_at(NY - dy, dc)

    def z_remote(step):
        to = row_of(step)
        slot = (z - to + NZ) % NZ - 1
        return pltpu.make_async_remote_copy(
            src_ref=zsend.at[step],
            dst_ref=zrecv.at[slot],
            send_sem=z_send.at[step],
            recv_sem=z_recv.at[slot],
            device_id=(to * NX + x, head),
            device_id_type=MESH,
        )

    def pass_on(step):
        for dx in range(1, NX):
            x_remote(step, dx).wait_recv()
        summed, total, peak = merged([xsend.at[step, x]] + [xrecv.at[step, dx] for dx in range(NX - 1)])
        summed, tail = pack(jnp.concatenate([summed, total], axis=0), peak)
        zsend[step, 0:HEAD_SIZE, :] = summed
        zsend[step, HEAD_SIZE:PART, :] = tail

        @pl.when(row_of(step) != z)
        def _():
            z_remote(step).start()

    def one_step(turn, first_step, last_step):
        step = label_at(turn)
        keys = FIRST_KC if first_step else KC
        queries = qt[turn % 2]
        if first_step:
            gather(0)
            scores = scores_of(0, keys, queries)
        else:
            scores = held[...]
        peak = acc = None
        for start in range(0, KEYS, keys):
            if start + keys < KEYS:
                if first_step:
                    gather(start // keys + 1)
                    if start == 2 * keys:
                        fetch(4)
                coming = scores_of(start + keys, keys, queries)
            elif not last_step:
                after = label_at(turn + 1)
                if first_step:
                    q_mate().wait_recv()
                else:
                    for k in range(2):
                        q_relay(after, k).wait_recv()
                following = turned(after)
                qt[(turn + 1) % 2] = following
                held[...] = scores_of(0, KC, following)
            best = jnp.max(scores, axis=0, keepdims=True)
            if start > 0:
                best = jnp.maximum(peak, best)
            best = best.astype(jnp.bfloat16).astype(jnp.float32)
            prob = jnp.exp2(scores - best).astype(jnp.bfloat16)
            added = jnp.dot(vt[:, start : start + keys], prob, preferred_element_type=jnp.float32)
            acc = added if start == 0 else acc * jnp.exp2(peak - best) + added
            peak = best
            scores = coming
            if last_step and start == 0:
                pass_on(label_at(turn - 2))
        summed, tail = pack(acc, peak)
        for part in range(NX):
            xsend[step, part, 0:HEAD_SIZE, :] = summed[:, part * 128 : (part + 1) * 128]
            xsend[step, part, HEAD_SIZE:PART, :] = tail[:, part * 128 : (part + 1) * 128]
        for dx in range(1, NX):
            x_remote(step, dx).start()

    local[4].wait()
    qt[0] = turned(0)
    one_step(0, True, False)
    fetch(5)
    fetch(6)
    forward(2)
    forward(3)

    def middle(turn, carry):
        one_step(turn, False, False)

        @pl.when(turn == 1)
        def _():
            fetch(7)
            forward(4)

        @pl.when(turn == 2)
        def _():
            forward(5)
            forward(6)

        @pl.when(turn == 3)
        def _():
            forward(7)

        @pl.when(turn > 1)
        def _():
            pass_on(label_at(turn - 2))

        return carry

    lax.fori_loop(1, NSTEP - 1, middle, 0)
    one_step(NSTEP - 1, False, True)
    for turn in range(NSTEP - 2, NSTEP):
        pass_on(label_at(turn))

    own_y = (y - z // 2 + NY) % NY
    own_step = step_of(own_y, (core + z) % 2)
    for slot in range(NZ - 1):
        pltpu.make_async_remote_copy(
            src_ref=zsend.at[0],
            dst_ref=zrecv.at[slot],
            send_sem=z_send.at[0],
            recv_sem=z_recv.at[slot],
            device_id=(ctx, head),
            device_id_type=MESH,
        ).wait_recv()
    summed, total, _ = merged([zsend.at[own_step]] + [zrecv.at[slot] for slot in range(NZ - 1)])
    out_ref[...] = (summed / total).T.reshape(out_ref.shape).astype(out_ref.dtype)

    q_mate().wait_send()

    def finish(step, carry):
        for dx in range(1, NX):
            x_remote(step, dx).wait_send()

        @pl.when(step > 1)
        def _():
            for k in range(2):
                q_direct(step, k).wait_send()
                q_relay(step, k).wait_send()

        @pl.when(row_of(step) != z)
        def _():
            z_remote(step).wait_send()

        return carry

    lax.fori_loop(0, NSTEP, finish, 0)


def on_device(queries, keys, values, key_block_scale, value_block_scale, selection):
    hbm = pl.BlockSpec(memory_space=pltpu.HBM)
    tokens = queries.shape[0]
    blocks = (keys.shape[1] // BLK, BLK, HEAD_SIZE)
    dma = pltpu.SemaphoreType.DMA
    return pl.pallas_call(
        kernel,
        out_shape=jax.ShapeDtypeStruct((tokens // NX, GROUP, HEAD_SIZE), jnp.bfloat16),
        in_specs=[hbm] * 6,
        out_specs=pl.BlockSpec(memory_space=pltpu.VMEM),
        scratch_shapes=[
            pltpu.VMEM(blocks, jnp.bfloat16),
            pltpu.VMEM(blocks, jnp.bfloat16),
            pltpu.VMEM((KEYS, 2 * HEAD_SIZE), jnp.bfloat16),
            pltpu.VMEM((PART, KEYS), jnp.bfloat16),
            pltpu.VMEM((NSTEP, tokens, GROUP, HEAD_SIZE), jnp.bfloat16),
            pltpu.VMEM((2, 2 * HEAD_SIZE, ROWS), jnp.bfloat16),
            pltpu.VMEM((KC, ROWS), jnp.float32),
            pltpu.VMEM((NSTEP, NX, PART, 128), jnp.bfloat16),
            pltpu.VMEM((NSTEP, NX - 1, PART, 128), jnp.bfloat16),
            pltpu.VMEM((NSTEP, PART, 128), jnp.bfloat16),
            pltpu.VMEM((NZ - 1, PART, 128), jnp.bfloat16),
            pltpu.SMEM((1, keys.shape[1] // BLK), jnp.float32),
            pltpu.SMEM((1, keys.shape[1] // BLK), jnp.float32),
            pltpu.SMEM(selection.shape, jnp.int32),
            pltpu.VMEM(selection.shape, jnp.int32),
            dma((9,)),
            dma((NSTEP, 4)),
            dma((NSTEP, 4)),
            dma((NSTEP, NX - 1)),
            dma((NSTEP, NX - 1)),
            dma((NSTEP,)),
            dma((NZ - 1,)),
        ],
        compiler_params=pltpu.CompilerParams(
            collective_id=0, has_side_effects=True, vmem_limit_bytes=60 << 20
        ),
    )(queries, keys.reshape(blocks), values.reshape(blocks), key_block_scale, value_block_scale, selection)


def solution(mesh):
    return jax.shard_map(
        on_device,
        mesh=mesh,
        in_specs=(
            P("head", None, None),
            P("head", "ctx", None),
            P("head", "ctx", None),
            P("head", "ctx"),
            P("head", "ctx"),
            P("head", None),
        ),
        out_specs=P("ctx", "head", None),
        check_vma=False,
    )
```

```python
import functools

import jax
import jax.numpy as jnp
from jax import lax
from jax.experimental import pallas as pl
from jax.experimental.pallas import tpu as pltpu
from jax.sharding import PartitionSpec as P

HEAD_SIZE = 128
BLK = 64
MOST = 40
GROUP = 16
KEYS = MOST * BLK
PART = 144
NZ, NX, NY = 8, 4, 4
NSTEP = 2 * NY
ROWS = 512
FIRST_KC, KC = 512, 1280
LOG2E = 1.4426950408889634
MESH = pl.DeviceIdType.MESH


def turn_of(step):
    far, k = (step + 6) // 8, (step + 4) % 6
    return far * (1 + 2 * (k % 3 % 2) + k % 3 // 2), far * (k // 3) + (1 - far) * step


def step_of(dy, dc):
    far = (dy + 3) // 4
    return dc + far * (2 + 2 * dc + (dy // 2) * (4 - dy))


def pack(acc, peak):
    total = acc[HEAD_SIZE : HEAD_SIZE + 1]
    high = total.astype(jnp.bfloat16).astype(jnp.float32)
    row = lax.broadcasted_iota(jnp.int32, (16, acc.shape[1]), 0)
    tail = jnp.where(row == 0, peak, jnp.where(row == 1, high, jnp.where(row == 2, total - high, 0.0)))
    return acc[:HEAD_SIZE].astype(jnp.bfloat16), tail.astype(jnp.bfloat16)


def merged(parts):
    tails = [part[HEAD_SIZE:PART, :].astype(jnp.float32) for part in parts]
    peak = functools.reduce(jnp.maximum, [tail[0:1] for tail in tails])
    total = jnp.zeros_like(peak)
    summed = jnp.zeros((HEAD_SIZE, 128), jnp.float32)
    for part, tail in zip(parts, tails):
        fade = jnp.exp2(tail[0:1] - peak)
        total = total + fade * (tail[1:2] + tail[2:3])
        summed = summed + fade * part[:HEAD_SIZE, :].astype(jnp.float32)
    return summed, total, peak


def kernel(
    q_hbm, k_hbm, v_hbm, ks_hbm, vs_hbm, sel_hbm, out_ref,
    kbuf, vbuf, kk, vt, qbuf, xsend, xrecv, zsend, zrecv, ks_ref, vs_ref, sel_ref, selv_ref,
    local_sem, q_send, q_recv, x_send, x_recv, z_send, z_recv,
):
    ctx = lax.axis_index("ctx")
    head = lax.axis_index("head")
    z, x = ctx // NX, ctx % NX
    y, core = head // 2, head % 2
    local_blocks = kbuf.shape[0]

    def head_at(dy, dc):
        return ((y + dy) % NY) * 2 + (core + dc) % 2

    local = [
        pltpu.make_async_copy(sel_hbm, selv_ref, local_sem.at[0]),
        pltpu.make_async_copy(sel_hbm, sel_ref, local_sem.at[1]),
        pltpu.make_async_copy(ks_hbm, ks_ref, local_sem.at[2]),
        pltpu.make_async_copy(vs_hbm, vs_ref, local_sem.at[3]),
        pltpu.make_async_copy(
            q_hbm.at[:, pl.ds(pl.multiple_of(head * GROUP, GROUP), GROUP), :], qbuf.at[0], local_sem.at[4]
        ),
    ]
    half = local_blocks // 2
    for k in range(2):
        part = pl.ds(k * half, half)
        local.append(pltpu.make_async_copy(k_hbm.at[part], kbuf.at[part], local_sem.at[5 + k]))
    for k in range(2):
        part = pl.ds(k * half, half)
        local.append(pltpu.make_async_copy(v_hbm.at[part], vbuf.at[part], local_sem.at[7 + k]))
    for copy in local:
        copy.start()

    barrier = pltpu.get_barrier_semaphore()
    for step in range(1, NSTEP):
        dy, dc = turn_of(step)
        pl.semaphore_signal(barrier, inc=1, device_id=(ctx, head_at(dy, dc)), device_id_type=MESH)
    for dx in range(1, NX):
        pl.semaphore_signal(barrier, inc=1, device_id=(z * NX + (x + dx) % NX, head), device_id_type=MESH)
    for dz in range(1, NZ):
        pl.semaphore_signal(barrier, inc=1, device_id=(((z + dz) % NZ) * NX + x, head), device_id_type=MESH)
    pl.semaphore_wait(barrier, NSTEP - 1 + NX - 1 + NZ - 1)

    def q_remote(step):
        dy, dc = turn_of(step)
        to = head_at(dy, dc)
        return pltpu.make_async_remote_copy(
            src_ref=q_hbm.at[:, pl.ds(pl.multiple_of(to * GROUP, GROUP), GROUP), :],
            dst_ref=qbuf.at[step],
            send_sem=q_send.at[step],
            recv_sem=q_recv.at[step],
            device_id=(ctx, to),
            device_id_type=MESH,
        )

    for step in range(1, 4):
        q_remote(step).start()

    for copy in local[:4]:
        copy.wait()
    base = ctx * local_blocks
    chosen = selv_ref[...]
    first = jnp.sum((chosen < base).astype(jnp.int32))
    last = jnp.sum((chosen < base + local_blocks).astype(jnp.int32)) - 1
    factor = LOG2E / HEAD_SIZE**0.5

    for copy in local[5:]:
        copy.wait()

    def gather(turn):
        for pair in range(turn * FIRST_KC // (2 * BLK), (turn + 1) * FIRST_KC // (2 * BLK)):
            value_parts = []
            mask_parts = []
            for side in range(2):
                j = first + pair * 2 + side
                place = jnp.maximum(jnp.minimum(j, last), 0)
                block = jnp.clip(sel_ref[0, place] - base, 0, local_blocks - 1)
                key_rows = kbuf[block].astype(jnp.float32) * (ks_ref[0, block] * factor)
                high = key_rows.astype(jnp.bfloat16)
                low = (key_rows - high.astype(jnp.float32)).astype(jnp.bfloat16)
                row = (pair * 2 + side) * BLK
                kk[row : row + BLK, 0:HEAD_SIZE] = high
                kk[row : row + BLK, HEAD_SIZE : 2 * HEAD_SIZE] = low
                live = jnp.where(j <= last, 1.0, 0.0)
                value_parts.append(vbuf[block].astype(jnp.float32) * (vs_ref[0, block] * live))
                mask_parts.append(live)
            values = jnp.concatenate(value_parts, axis=0).astype(jnp.bfloat16).T
            column = pl.ds(pair * 2 * BLK, 2 * BLK)
            vt[0:HEAD_SIZE, column] = values
            lane = lax.broadcasted_iota(jnp.int32, (16, 2 * BLK), 1)
            vt[HEAD_SIZE:PART, column] = jnp.where(lane < BLK, mask_parts[0], mask_parts[1]).astype(jnp.bfloat16)

    def turned(step):
        flat = qbuf[step].reshape(ROWS, HEAD_SIZE).T
        return jnp.concatenate([flat, flat], axis=0)

    def scores_of(start, keys, queries):
        return jnp.dot(kk[start : start + keys, :], queries, preferred_element_type=jnp.float32)

    def x_remote(step, dx):
        to = (x + dx) % NX
        return pltpu.make_async_remote_copy(
            src_ref=xsend.at[step, to],
            dst_ref=xrecv.at[step, dx - 1],
            send_sem=x_send.at[step, dx - 1],
            recv_sem=x_recv.at[step, dx - 1],
            device_id=(z * NX + to, head),
            device_id_type=MESH,
        )

    def row_of(step):
        dy, dc = turn_of(step)
        return head_at(NY - dy, dc)

    def z_remote(step):
        to = row_of(step)
        slot = (z - to + NZ) % NZ - 1
        return pltpu.make_async_remote_copy(
            src_ref=zsend.at[step],
            dst_ref=zrecv.at[slot],
            send_sem=z_send.at[step],
            recv_sem=z_recv.at[slot],
            device_id=(to * NX + x, head),
            device_id_type=MESH,
        )

    def pass_on(step):
        for dx in range(1, NX):
            x_remote(step, dx).wait_recv()
        summed, total, peak = merged([xsend.at[step, x]] + [xrecv.at[step, dx] for dx in range(NX - 1)])
        summed, tail = pack(jnp.concatenate([summed, total], axis=0), peak)
        zsend[step, 0:HEAD_SIZE, :] = summed
        zsend[step, HEAD_SIZE:PART, :] = tail

        @pl.when(row_of(step) != z)
        def _():
            z_remote(step).start()

    def one_step(step, first_step):
        keys = FIRST_KC if first_step else KC
        queries = turned(step)
        if first_step:
            gather(0)
        scores = scores_of(0, keys, queries)
        peak = acc = None
        for start in range(0, KEYS, keys):
            if start + keys < KEYS:
                if first_step:
                    gather(start // keys + 1)
                coming = scores_of(start + keys, keys, queries)
            best = jnp.max(scores, axis=0, keepdims=True)
            if start > 0:
                best = jnp.maximum(peak, best)
            best = best.astype(jnp.bfloat16).astype(jnp.float32)
            prob = jnp.exp2(scores - best).astype(jnp.bfloat16)
            added = jnp.dot(vt[:, start : start + keys], prob, preferred_element_type=jnp.float32)
            acc = added if start == 0 else acc * jnp.exp2(peak - best) + added
            peak = best
            scores = coming
        summed, tail = pack(acc, peak)
        for part in range(NX):
            xsend[step, part, 0:HEAD_SIZE, :] = summed[:, part * 128 : (part + 1) * 128]
            xsend[step, part, HEAD_SIZE:PART, :] = tail[:, part * 128 : (part + 1) * 128]
        for dx in range(1, NX):
            x_remote(step, dx).start()

    local[4].wait()
    q_remote(4).start()
    one_step(0, True)

    def later(step, carry):
        @pl.when(step < 4)
        def _():
            q_remote(step + 4).start()

        q_remote(step).wait_recv()
        one_step(step, False)

        @pl.when(step > 1)
        def _():
            pass_on(step - 2)

        return carry

    lax.fori_loop(1, NSTEP, later, 0)
    for step in range(NSTEP - 2, NSTEP):
        pass_on(step)

    own_y = (y - z // 2 + NY) % NY
    own_step = step_of(own_y, (core + z) % 2)
    for slot in range(NZ - 1):
        pltpu.make_async_remote_copy(
            src_ref=zsend.at[0],
            dst_ref=zrecv.at[slot],
            send_sem=z_send.at[0],
            recv_sem=z_recv.at[slot],
            device_id=(ctx, head),
            device_id_type=MESH,
        ).wait_recv()
    summed, total, _ = merged([zsend.at[own_step]] + [zrecv.at[slot] for slot in range(NZ - 1)])
    out_ref[...] = (summed / total).T.reshape(out_ref.shape).astype(out_ref.dtype)

    def finish(step, carry):
        for dx in range(1, NX):
            x_remote(step, dx).wait_send()

        @pl.when(step > 0)
        def _():
            q_remote(step).wait_send()

        @pl.when(row_of(step) != z)
        def _():
            z_remote(step).wait_send()

        return carry

    lax.fori_loop(0, NSTEP, finish, 0)


def on_device(queries, keys, values, key_block_scale, value_block_scale, selection):
    hbm = pl.BlockSpec(memory_space=pltpu.HBM)
    tokens = queries.shape[0]
    blocks = (keys.shape[1] // BLK, BLK, HEAD_SIZE)
    dma = pltpu.SemaphoreType.DMA
    return pl.pallas_call(
        kernel,
        out_shape=jax.ShapeDtypeStruct((tokens // NX, GROUP, HEAD_SIZE), jnp.bfloat16),
        in_specs=[hbm] * 6,
        out_specs=pl.BlockSpec(memory_space=pltpu.VMEM),
        scratch_shapes=[
            pltpu.VMEM(blocks, jnp.bfloat16),
            pltpu.VMEM(blocks, jnp.bfloat16),
            pltpu.VMEM((KEYS, 2 * HEAD_SIZE), jnp.bfloat16),
            pltpu.VMEM((PART, KEYS), jnp.bfloat16),
            pltpu.VMEM((NSTEP, tokens, GROUP, HEAD_SIZE), jnp.bfloat16),
            pltpu.VMEM((NSTEP, NX, PART, 128), jnp.bfloat16),
            pltpu.VMEM((NSTEP, NX - 1, PART, 128), jnp.bfloat16),
            pltpu.VMEM((NSTEP, PART, 128), jnp.bfloat16),
            pltpu.VMEM((NZ - 1, PART, 128), jnp.bfloat16),
            pltpu.SMEM((1, keys.shape[1] // BLK), jnp.float32),
            pltpu.SMEM((1, keys.shape[1] // BLK), jnp.float32),
            pltpu.SMEM(selection.shape, jnp.int32),
            pltpu.VMEM(selection.shape, jnp.int32),
            dma((9,)),
            dma((NSTEP,)),
            dma((NSTEP,)),
            dma((NSTEP, NX - 1)),
            dma((NSTEP, NX - 1)),
            dma((NSTEP,)),
            dma((NZ - 1,)),
        ],
        compiler_params=pltpu.CompilerParams(
            collective_id=0, has_side_effects=True, vmem_limit_bytes=60 << 20
        ),
    )(queries, keys.reshape(blocks), values.reshape(blocks), key_block_scale, value_block_scale, selection)


def solution(mesh):
    return jax.shard_map(
        on_device,
        mesh=mesh,
        in_specs=(
            P("head", None, None),
            P("head", "ctx", None),
            P("head", "ctx", None),
            P("head", "ctx"),
            P("head", "ctx"),
            P("head", None),
        ),
        out_specs=P("ctx", "head", None),
        check_vma=False,
    )
```

```python
import functools

import jax
import jax.numpy as jnp
from jax import lax
from jax.experimental import pallas as pl
from jax.experimental.pallas import tpu as pltpu
from jax.sharding import PartitionSpec as P

HEAD_SIZE = 128
BLK = 64
MOST = 40
GROUP = 16
KEYS = MOST * BLK
PART = 144
NZ, NX, NY = 8, 4, 4
NSTEP = 2 * NY
ROWS = 512
FIRST_KC, KC = 512, 1280
LOG2E = 1.4426950408889634
MESH = pl.DeviceIdType.MESH


def turn_of(step):
    far, k = (step + 6) // 8, (step + 4) % 6
    return far * (1 + 2 * (k % 3 % 2) + k % 3 // 2), far * (k // 3) + (1 - far) * step


def step_of(dy, dc):
    far = (dy + 3) // 4
    return dc + far * (2 + 2 * dc + (dy // 2) * (4 - dy))


def pack(acc, peak):
    total = acc[HEAD_SIZE : HEAD_SIZE + 1]
    high = total.astype(jnp.bfloat16).astype(jnp.float32)
    row = lax.broadcasted_iota(jnp.int32, (16, acc.shape[1]), 0)
    tail = jnp.where(row == 0, peak, jnp.where(row == 1, high, jnp.where(row == 2, total - high, 0.0)))
    return acc[:HEAD_SIZE].astype(jnp.bfloat16), tail.astype(jnp.bfloat16)


def merged(parts):
    tails = [part[HEAD_SIZE:PART, :].astype(jnp.float32) for part in parts]
    peak = functools.reduce(jnp.maximum, [tail[0:1] for tail in tails])
    total = jnp.zeros_like(peak)
    summed = jnp.zeros((HEAD_SIZE, 128), jnp.float32)
    for part, tail in zip(parts, tails):
        fade = jnp.exp2(tail[0:1] - peak)
        total = total + fade * (tail[1:2] + tail[2:3])
        summed = summed + fade * part[:HEAD_SIZE, :].astype(jnp.float32)
    return summed, total, peak


def kernel(
    q_hbm, k_hbm, v_hbm, ks_hbm, vs_hbm, sel_hbm, out_ref,
    kbuf, vbuf, kk, vt, qbuf, xsend, xrecv, zsend, zrecv, ks_ref, vs_ref, sel_ref, selv_ref,
    local_sem, q_send, q_recv, x_send, x_recv, z_send, z_recv,
):
    ctx = lax.axis_index("ctx")
    head = lax.axis_index("head")
    z, x = ctx // NX, ctx % NX
    y, core = head // 2, head % 2
    local_blocks = kbuf.shape[0]

    def head_at(dy, dc):
        return ((y + dy) % NY) * 2 + (core + dc) % 2

    barrier = pltpu.get_barrier_semaphore()

    def greet(to):
        pl.semaphore_signal(barrier, inc=1, device_id=to, device_id_type=MESH)

    for dz in (4, 3, 5, 2, 6):
        greet((((z + dz) % NZ) * NX + x, head))
    for step in (4, 7):
        dy, dc = turn_of(step)
        greet((ctx, head_at(dy, dc)))
    greet((z * NX + (x + 2) % NX, head))
    for step in (2, 3, 5, 6, 1):
        dy, dc = turn_of(step)
        greet((ctx, head_at(dy, dc)))
    for dx in (1, 3):
        greet((z * NX + (x + dx) % NX, head))
    for dz in (1, 7):
        greet((((z + dz) % NZ) * NX + x, head))

    local = [
        pltpu.make_async_copy(sel_hbm, selv_ref, local_sem.at[0]),
        pltpu.make_async_copy(sel_hbm, sel_ref, local_sem.at[1]),
        pltpu.make_async_copy(ks_hbm, ks_ref, local_sem.at[2]),
        pltpu.make_async_copy(vs_hbm, vs_ref, local_sem.at[3]),
        pltpu.make_async_copy(
            q_hbm.at[:, pl.ds(pl.multiple_of(head * GROUP, GROUP), GROUP), :], qbuf.at[0], local_sem.at[4]
        ),
    ]
    half = local_blocks // 2
    for k in range(2):
        part = pl.ds(k * half, half)
        local.append(pltpu.make_async_copy(k_hbm.at[part], kbuf.at[part], local_sem.at[5 + k]))
    for k in range(2):
        part = pl.ds(k * half, half)
        local.append(pltpu.make_async_copy(v_hbm.at[part], vbuf.at[part], local_sem.at[7 + k]))
    for copy in local:
        copy.start()

    pl.semaphore_wait(barrier, NSTEP - 1 + NX - 1 + NZ - 1)

    def q_remote(step):
        dy, dc = turn_of(step)
        to = head_at(dy, dc)
        return pltpu.make_async_remote_copy(
            src_ref=q_hbm.at[:, pl.ds(pl.multiple_of(to * GROUP, GROUP), GROUP), :],
            dst_ref=qbuf.at[step],
            send_sem=q_send.at[step],
            recv_sem=q_recv.at[step],
            device_id=(ctx, to),
            device_id_type=MESH,
        )

    for step in range(1, 4):
        q_remote(step).start()

    for copy in local[:4]:
        copy.wait()
    base = ctx * local_blocks
    chosen = selv_ref[...]
    first = jnp.sum((chosen < base).astype(jnp.int32))
    last = jnp.sum((chosen < base + local_blocks).astype(jnp.int32)) - 1
    factor = LOG2E / HEAD_SIZE**0.5

    for copy in local[5:]:
        copy.wait()

    def gather(turn):
        for pair in range(turn * FIRST_KC // (2 * BLK), (turn + 1) * FIRST_KC // (2 * BLK)):
            value_parts = []
            mask_parts = []
            for side in range(2):
                j = first + pair * 2 + side
                place = jnp.maximum(jnp.minimum(j, last), 0)
                block = jnp.clip(sel_ref[0, place] - base, 0, local_blocks - 1)
                key_rows = kbuf[block].astype(jnp.float32) * (ks_ref[0, block] * factor)
                high = key_rows.astype(jnp.bfloat16)
                low = (key_rows - high.astype(jnp.float32)).astype(jnp.bfloat16)
                row = (pair * 2 + side) * BLK
                kk[row : row + BLK, 0:HEAD_SIZE] = high
                kk[row : row + BLK, HEAD_SIZE : 2 * HEAD_SIZE] = low
                live = jnp.where(j <= last, 1.0, 0.0)
                value_parts.append(vbuf[block].astype(jnp.float32) * (vs_ref[0, block] * live))
                mask_parts.append(live)
            values = jnp.concatenate(value_parts, axis=0).astype(jnp.bfloat16).T
            column = pl.ds(pair * 2 * BLK, 2 * BLK)
            vt[0:HEAD_SIZE, column] = values
            lane = lax.broadcasted_iota(jnp.int32, (16, 2 * BLK), 1)
            vt[HEAD_SIZE:PART, column] = jnp.where(lane < BLK, mask_parts[0], mask_parts[1]).astype(jnp.bfloat16)

    def turned(step):
        flat = qbuf[step].reshape(ROWS, HEAD_SIZE).T
        return jnp.concatenate([flat, flat], axis=0)

    def scores_of(start, keys, queries):
        return jnp.dot(kk[start : start + keys, :], queries, preferred_element_type=jnp.float32)

    def x_remote(step, dx):
        to = (x + dx) % NX
        return pltpu.make_async_remote_copy(
            src_ref=xsend.at[step, to],
            dst_ref=xrecv.at[step, dx - 1],
            send_sem=x_send.at[step, dx - 1],
            recv_sem=x_recv.at[step, dx - 1],
            device_id=(z * NX + to, head),
            device_id_type=MESH,
        )

    def row_of(step):
        dy, dc = turn_of(step)
        return head_at(NY - dy, dc)

    def z_remote(step):
        to = row_of(step)
        slot = (z - to + NZ) % NZ - 1
        return pltpu.make_async_remote_copy(
            src_ref=zsend.at[step],
            dst_ref=zrecv.at[slot],
            send_sem=z_send.at[step],
            recv_sem=z_recv.at[slot],
            device_id=(to * NX + x, head),
            device_id_type=MESH,
        )

    def pass_on(step):
        for dx in range(1, NX):
            x_remote(step, dx).wait_recv()
        summed, total, peak = merged([xsend.at[step, x]] + [xrecv.at[step, dx] for dx in range(NX - 1)])
        summed, tail = pack(jnp.concatenate([summed, total], axis=0), peak)
        zsend[step, 0:HEAD_SIZE, :] = summed
        zsend[step, HEAD_SIZE:PART, :] = tail

        @pl.when(row_of(step) != z)
        def _():
            z_remote(step).start()

    def one_step(step, first_step):
        keys = FIRST_KC if first_step else KC
        queries = turned(step)
        if first_step:
            gather(0)
        scores = scores_of(0, keys, queries)
        peak = acc = None
        for start in range(0, KEYS, keys):
            if start + keys < KEYS:
                if first_step:
                    gather(start // keys + 1)
                coming = scores_of(start + keys, keys, queries)
            best = jnp.max(scores, axis=0, keepdims=True)
            if start > 0:
                best = jnp.maximum(peak, best)
            best = best.astype(jnp.bfloat16).astype(jnp.float32)
            prob = jnp.exp2(scores - best).astype(jnp.bfloat16)
            added = jnp.dot(vt[:, start : start + keys], prob, preferred_element_type=jnp.float32)
            acc = added if start == 0 else acc * jnp.exp2(peak - best) + added
            peak = best
            scores = coming
        summed, tail = pack(acc, peak)
        for part in range(NX):
            xsend[step, part, 0:HEAD_SIZE, :] = summed[:, part * 128 : (part + 1) * 128]
            xsend[step, part, HEAD_SIZE:PART, :] = tail[:, part * 128 : (part + 1) * 128]
        for dx in (2, 1, 3):
            x_remote(step, dx).start()

    local[4].wait()
    one_step(0, True)

    def later(step, carry):
        @pl.when(step < 4)
        def _():
            q_remote(step + 3 + step // 3).start()

        @pl.when(step == 2)
        def _():
            q_remote(6).start()

        q_remote(step).wait_recv()
        one_step(step, False)

        @pl.when(step > 1)
        def _():
            pass_on(step - 2)

        return carry

    lax.fori_loop(1, NSTEP, later, 0)
    for step in range(NSTEP - 2, NSTEP):
        pass_on(step)

    own_y = (y - z // 2 + NY) % NY
    own_step = step_of(own_y, (core + z) % 2)
    for slot in range(NZ - 1):
        pltpu.make_async_remote_copy(
            src_ref=zsend.at[0],
            dst_ref=zrecv.at[slot],
            send_sem=z_send.at[0],
            recv_sem=z_recv.at[slot],
            device_id=(ctx, head),
            device_id_type=MESH,
        ).wait_recv()
    summed, total, _ = merged([zsend.at[own_step]] + [zrecv.at[slot] for slot in range(NZ - 1)])
    out_ref[...] = (summed / total).T.reshape(out_ref.shape).astype(out_ref.dtype)

    def finish(step, carry):
        for dx in range(1, NX):
            x_remote(step, dx).wait_send()

        @pl.when(step > 0)
        def _():
            q_remote(step).wait_send()

        @pl.when(row_of(step) != z)
        def _():
            z_remote(step).wait_send()

        return carry

    lax.fori_loop(0, NSTEP, finish, 0)


def on_device(queries, keys, values, key_block_scale, value_block_scale, selection):
    hbm = pl.BlockSpec(memory_space=pltpu.HBM)
    tokens = queries.shape[0]
    blocks = (keys.shape[1] // BLK, BLK, HEAD_SIZE)
    dma = pltpu.SemaphoreType.DMA
    return pl.pallas_call(
        kernel,
        out_shape=jax.ShapeDtypeStruct((tokens // NX, GROUP, HEAD_SIZE), jnp.bfloat16),
        in_specs=[hbm] * 6,
        out_specs=pl.BlockSpec(memory_space=pltpu.VMEM),
        scratch_shapes=[
            pltpu.VMEM(blocks, jnp.bfloat16),
            pltpu.VMEM(blocks, jnp.bfloat16),
            pltpu.VMEM((KEYS, 2 * HEAD_SIZE), jnp.bfloat16),
            pltpu.VMEM((PART, KEYS), jnp.bfloat16),
            pltpu.VMEM((NSTEP, tokens, GROUP, HEAD_SIZE), jnp.bfloat16),
            pltpu.VMEM((NSTEP, NX, PART, 128), jnp.bfloat16),
            pltpu.VMEM((NSTEP, NX - 1, PART, 128), jnp.bfloat16),
            pltpu.VMEM((NSTEP, PART, 128), jnp.bfloat16),
            pltpu.VMEM((NZ - 1, PART, 128), jnp.bfloat16),
            pltpu.SMEM((1, keys.shape[1] // BLK), jnp.float32),
            pltpu.SMEM((1, keys.shape[1] // BLK), jnp.float32),
            pltpu.SMEM(selection.shape, jnp.int32),
            pltpu.VMEM(selection.shape, jnp.int32),
            dma((9,)),
            dma((NSTEP,)),
            dma((NSTEP,)),
            dma((NSTEP, NX - 1)),
            dma((NSTEP, NX - 1)),
            dma((NSTEP,)),
            dma((NZ - 1,)),
        ],
        compiler_params=pltpu.CompilerParams(
            collective_id=0, has_side_effects=True, vmem_limit_bytes=60 << 20
        ),
    )(queries, keys.reshape(blocks), values.reshape(blocks), key_block_scale, value_block_scale, selection)


def solution(mesh):
    return jax.shard_map(
        on_device,
        mesh=mesh,
        in_specs=(
            P("head", None, None),
            P("head", "ctx", None),
            P("head", "ctx", None),
            P("head", "ctx"),
            P("head", "ctx"),
            P("head", None),
        ),
        out_specs=P("ctx", "head", None),
        check_vma=False,
    )
```

```python
import functools

import jax
import jax.numpy as jnp
from jax import lax
from jax.experimental import pallas as pl
from jax.experimental.pallas import tpu as pltpu
from jax.sharding import PartitionSpec as P

HEAD_SIZE = 128
BLK = 64
MOST = 40
GROUP = 16
KEYS = MOST * BLK
PART = 144
NZ, NX, NY = 8, 4, 4
NSTEP = 2 * NY
ROWS = 512
FIRST_KC, KC = 512, 1280
LOG2E = 1.4426950408889634
MESH = pl.DeviceIdType.MESH


def turn_of(step):
    far, k = (step + 6) // 8, (step + 4) % 6
    return far * (1 + 2 * (k % 3 % 2) + k % 3 // 2), far * (k // 3) + (1 - far) * step


def step_of(dy, dc):
    far = (dy + 3) // 4
    return dc + far * (2 + 2 * dc + (dy // 2) * (4 - dy))


def pack(acc, peak):
    total = acc[HEAD_SIZE : HEAD_SIZE + 1]
    high = total.astype(jnp.bfloat16).astype(jnp.float32)
    row = lax.broadcasted_iota(jnp.int32, (16, acc.shape[1]), 0)
    tail = jnp.where(row == 0, peak, jnp.where(row == 1, high, jnp.where(row == 2, total - high, 0.0)))
    return acc[:HEAD_SIZE].astype(jnp.bfloat16), tail.astype(jnp.bfloat16)


def merged(parts):
    tails = [part[HEAD_SIZE:PART, :].astype(jnp.float32) for part in parts]
    peak = functools.reduce(jnp.maximum, [tail[0:1] for tail in tails])
    total = jnp.zeros_like(peak)
    summed = jnp.zeros((HEAD_SIZE, 128), jnp.float32)
    for part, tail in zip(parts, tails):
        fade = jnp.exp2(tail[0:1] - peak)
        total = total + fade * (tail[1:2] + tail[2:3])
        summed = summed + fade * part[:HEAD_SIZE, :].astype(jnp.float32)
    return summed, total, peak


def kernel(
    q_hbm, k_hbm, v_hbm, ks_hbm, vs_hbm, sel_hbm, out_ref,
    kbuf, vbuf, kk, vt, qbuf, xsend, xrecv, zsend, zrecv, ks_ref, vs_ref, sel_ref, selv_ref,
    local_sem, q_send, q_recv, x_send, x_recv, z_send, z_recv,
):
    ctx = lax.axis_index("ctx")
    head = lax.axis_index("head")
    z, x = ctx // NX, ctx % NX
    y, core = head // 2, head % 2
    local_blocks = kbuf.shape[0]

    def head_at(dy, dc):
        return ((y + dy) % NY) * 2 + (core + dc) % 2

    barrier = pltpu.get_barrier_semaphore()

    def greet(to):
        pl.semaphore_signal(barrier, inc=1, device_id=to, device_id_type=MESH)

    for dz in (4, 3, 5, 2, 6):
        greet((((z + dz) % NZ) * NX + x, head))
    for step in (4, 7):
        dy, dc = turn_of(step)
        greet((ctx, head_at(dy, dc)))
    greet((z * NX + (x + 2) % NX, head))
    for step in (2, 3, 5, 6, 1):
        dy, dc = turn_of(step)
        greet((ctx, head_at(dy, dc)))
    for dx in (1, 3):
        greet((z * NX + (x + dx) % NX, head))
    for dz in (1, 7):
        greet((((z + dz) % NZ) * NX + x, head))

    local = [
        pltpu.make_async_copy(sel_hbm, selv_ref, local_sem.at[0]),
        pltpu.make_async_copy(sel_hbm, sel_ref, local_sem.at[1]),
        pltpu.make_async_copy(ks_hbm, ks_ref, local_sem.at[2]),
        pltpu.make_async_copy(vs_hbm, vs_ref, local_sem.at[3]),
        pltpu.make_async_copy(
            q_hbm.at[:, pl.ds(pl.multiple_of(head * GROUP, GROUP), GROUP), :], qbuf.at[0], local_sem.at[4]
        ),
    ]
    half = local_blocks // 2
    for k in range(2):
        part = pl.ds(k * half, half)
        local.append(pltpu.make_async_copy(k_hbm.at[part], kbuf.at[part], local_sem.at[5 + k]))
    for k in range(2):
        part = pl.ds(k * half, half)
        local.append(pltpu.make_async_copy(v_hbm.at[part], vbuf.at[part], local_sem.at[7 + k]))
    for copy in local:
        copy.start()

    pl.semaphore_wait(barrier, NSTEP - 1 + NX - 1 + NZ - 1)

    def q_remote(step):
        dy, dc = turn_of(step)
        to = head_at(dy, dc)
        return pltpu.make_async_remote_copy(
            src_ref=q_hbm.at[:, pl.ds(pl.multiple_of(to * GROUP, GROUP), GROUP), :],
            dst_ref=qbuf.at[step],
            send_sem=q_send.at[step],
            recv_sem=q_recv.at[step],
            device_id=(ctx, to),
            device_id_type=MESH,
        )

    for step in range(1, 4):
        q_remote(step).start()

    for copy in local[:4]:
        copy.wait()
    base = ctx * local_blocks
    chosen = selv_ref[...]
    first = jnp.sum((chosen < base).astype(jnp.int32))
    last = jnp.sum((chosen < base + local_blocks).astype(jnp.int32)) - 1
    factor = LOG2E / HEAD_SIZE**0.5

    for copy in local[5:]:
        copy.wait()

    def gather(turn):
        for pair in range(turn * FIRST_KC // (2 * BLK), (turn + 1) * FIRST_KC // (2 * BLK)):
            value_parts = []
            mask_parts = []
            for side in range(2):
                j = first + pair * 2 + side
                place = jnp.maximum(jnp.minimum(j, last), 0)
                block = jnp.clip(sel_ref[0, place] - base, 0, local_blocks - 1)
                key_rows = kbuf[block].astype(jnp.float32) * (ks_ref[0, block] * factor)
                high = key_rows.astype(jnp.bfloat16)
                low = (key_rows - high.astype(jnp.float32)).astype(jnp.bfloat16)
                row = (pair * 2 + side) * BLK
                kk[row : row + BLK, 0:HEAD_SIZE] = high
                kk[row : row + BLK, HEAD_SIZE : 2 * HEAD_SIZE] = low
                live = jnp.where(j <= last, 1.0, 0.0)
                value_parts.append(vbuf[block].astype(jnp.float32) * (vs_ref[0, block] * live))
                mask_parts.append(live)
            values = jnp.concatenate(value_parts, axis=0).astype(jnp.bfloat16).T
            column = pl.ds(pair * 2 * BLK, 2 * BLK)
            vt[0:HEAD_SIZE, column] = values
            lane = lax.broadcasted_iota(jnp.int32, (16, 2 * BLK), 1)
            vt[HEAD_SIZE:PART, column] = jnp.where(lane < BLK, mask_parts[0], mask_parts[1]).astype(jnp.bfloat16)

    def turned(step):
        flat = qbuf[step].reshape(ROWS, HEAD_SIZE).T
        return jnp.concatenate([flat, flat], axis=0)

    def scores_of(start, keys, queries):
        return jnp.dot(kk[start : start + keys, :], queries, preferred_element_type=jnp.float32)

    def x_remote(step, dx):
        to = (x + dx) % NX
        return pltpu.make_async_remote_copy(
            src_ref=xsend.at[step, to],
            dst_ref=xrecv.at[step, dx - 1],
            send_sem=x_send.at[step, dx - 1],
            recv_sem=x_recv.at[step, dx - 1],
            device_id=(z * NX + to, head),
            device_id_type=MESH,
        )

    def row_of(step):
        dy, dc = turn_of(step)
        return head_at(NY - dy, dc)

    def z_remote(step):
        to = row_of(step)
        slot = (z - to + NZ) % NZ - 1
        return pltpu.make_async_remote_copy(
            src_ref=zsend.at[step],
            dst_ref=zrecv.at[slot],
            send_sem=z_send.at[step],
            recv_sem=z_recv.at[slot],
            device_id=(to * NX + x, head),
            device_id_type=MESH,
        )

    def pass_on(step):
        for dx in range(1, NX):
            x_remote(step, dx).wait_recv()
        summed, total, peak = merged([xsend.at[step, x]] + [xrecv.at[step, dx] for dx in range(NX - 1)])
        summed, tail = pack(jnp.concatenate([summed, total], axis=0), peak)
        zsend[step, 0:HEAD_SIZE, :] = summed
        zsend[step, HEAD_SIZE:PART, :] = tail

        @pl.when(row_of(step) != z)
        def _():
            z_remote(step).start()

    def one_step(step, first_step):
        keys = FIRST_KC if first_step else KC
        queries = turned(step)
        if first_step:
            gather(0)
        scores = scores_of(0, keys, queries)
        peak = acc = None
        for start in range(0, KEYS, keys):
            if start + keys < KEYS:
                if first_step:
                    gather(start // keys + 1)
                coming = scores_of(start + keys, keys, queries)
            best = jnp.max(scores, axis=0, keepdims=True)
            if start > 0:
                best = jnp.maximum(peak, best)
            best = best.astype(jnp.bfloat16).astype(jnp.float32)
            prob = jnp.exp2(scores - best).astype(jnp.bfloat16)
            added = jnp.dot(vt[:, start : start + keys], prob, preferred_element_type=jnp.float32)
            acc = added if start == 0 else acc * jnp.exp2(peak - best) + added
            peak = best
            scores = coming
        summed, tail = pack(acc, peak)
        for part in range(NX):
            xsend[step, part, 0:HEAD_SIZE, :] = summed[:, part * 128 : (part + 1) * 128]
            xsend[step, part, HEAD_SIZE:PART, :] = tail[:, part * 128 : (part + 1) * 128]
        for dx in (2, 1, 3):
            x_remote(step, dx).start()

    local[4].wait()
    one_step(0, True)

    def later(step, carry):
        @pl.when(step < 4)
        def _():
            q_remote(step + 3 + step // 3).start()

        @pl.when(step == 2)
        def _():
            q_remote(6).start()

        q_remote(step).wait_recv()
        one_step(step, False)

        @pl.when(step > 2)
        def _():
            pass_on(step - 3)

        return carry

    lax.fori_loop(1, NSTEP, later, 0)
    for step in range(NSTEP - 3, NSTEP):
        pass_on(step)

    own_y = (y - z // 2 + NY) % NY
    own_step = step_of(own_y, (core + z) % 2)
    for slot in range(NZ - 1):
        pltpu.make_async_remote_copy(
            src_ref=zsend.at[0],
            dst_ref=zrecv.at[slot],
            send_sem=z_send.at[0],
            recv_sem=z_recv.at[slot],
            device_id=(ctx, head),
            device_id_type=MESH,
        ).wait_recv()
    summed, total, _ = merged([zsend.at[own_step]] + [zrecv.at[slot] for slot in range(NZ - 1)])
    out_ref[...] = (summed / total).T.reshape(out_ref.shape).astype(out_ref.dtype)

    def finish(step, carry):
        for dx in range(1, NX):
            x_remote(step, dx).wait_send()

        @pl.when(step > 0)
        def _():
            q_remote(step).wait_send()

        @pl.when(row_of(step) != z)
        def _():
            z_remote(step).wait_send()

        return carry

    lax.fori_loop(0, NSTEP, finish, 0)


def on_device(queries, keys, values, key_block_scale, value_block_scale, selection):
    hbm = pl.BlockSpec(memory_space=pltpu.HBM)
    tokens = queries.shape[0]
    blocks = (keys.shape[1] // BLK, BLK, HEAD_SIZE)
    dma = pltpu.SemaphoreType.DMA
    return pl.pallas_call(
        kernel,
        out_shape=jax.ShapeDtypeStruct((tokens // NX, GROUP, HEAD_SIZE), jnp.bfloat16),
        in_specs=[hbm] * 6,
        out_specs=pl.BlockSpec(memory_space=pltpu.VMEM),
        scratch_shapes=[
            pltpu.VMEM(blocks, jnp.bfloat16),
            pltpu.VMEM(blocks, jnp.bfloat16),
            pltpu.VMEM((KEYS, 2 * HEAD_SIZE), jnp.bfloat16),
            pltpu.VMEM((PART, KEYS), jnp.bfloat16),
            pltpu.VMEM((NSTEP, tokens, GROUP, HEAD_SIZE), jnp.bfloat16),
            pltpu.VMEM((NSTEP, NX, PART, 128), jnp.bfloat16),
            pltpu.VMEM((NSTEP, NX - 1, PART, 128), jnp.bfloat16),
            pltpu.VMEM((NSTEP, PART, 128), jnp.bfloat16),
            pltpu.VMEM((NZ - 1, PART, 128), jnp.bfloat16),
            pltpu.SMEM((1, keys.shape[1] // BLK), jnp.float32),
            pltpu.SMEM((1, keys.shape[1] // BLK), jnp.float32),
            pltpu.SMEM(selection.shape, jnp.int32),
            pltpu.VMEM(selection.shape, jnp.int32),
            dma((9,)),
            dma((NSTEP,)),
            dma((NSTEP,)),
            dma((NSTEP, NX - 1)),
            dma((NSTEP, NX - 1)),
            dma((NSTEP,)),
            dma((NZ - 1,)),
        ],
        compiler_params=pltpu.CompilerParams(
            collective_id=0, has_side_effects=True, vmem_limit_bytes=60 << 20
        ),
    )(queries, keys.reshape(blocks), values.reshape(blocks), key_block_scale, value_block_scale, selection)


def solution(mesh):
    return jax.shard_map(
        on_device,
        mesh=mesh,
        in_specs=(
            P("head", None, None),
            P("head", "ctx", None),
            P("head", "ctx", None),
            P("head", "ctx"),
            P("head", "ctx"),
            P("head", None),
        ),
        out_specs=P("ctx", "head", None),
        check_vma=False,
    )
```

```python
import functools

import jax
import jax.numpy as jnp
from jax import lax
from jax.experimental import pallas as pl
from jax.experimental.pallas import tpu as pltpu
from jax.sharding import PartitionSpec as P

HEAD_SIZE = 128
BLK = 64
MOST = 40
GROUP = 16
KEYS = MOST * BLK
PART = 144
NZ, NX, NY = 8, 4, 4
NSTEP = 2 * NY
ROWS = 512
FIRST_KC, KC = 512, 1280
LOG2E = 1.4426950408889634
MESH = pl.DeviceIdType.MESH


def turn_of(step):
    far, k = (step + 6) // 8, (step + 4) % 6
    return far * (1 + 2 * (k % 3 % 2) + k % 3 // 2), far * (k // 3) + (1 - far) * step


def step_of(dy, dc):
    far = (dy + 3) // 4
    return dc + far * (2 + 2 * dc + (dy // 2) * (4 - dy))


def pack(acc, peak):
    total = acc[HEAD_SIZE : HEAD_SIZE + 1]
    high = total.astype(jnp.bfloat16).astype(jnp.float32)
    row = lax.broadcasted_iota(jnp.int32, (16, acc.shape[1]), 0)
    tail = jnp.where(row == 0, peak, jnp.where(row == 1, high, jnp.where(row == 2, total - high, 0.0)))
    return acc[:HEAD_SIZE].astype(jnp.bfloat16), tail.astype(jnp.bfloat16)


def merged(parts):
    tails = [part[HEAD_SIZE:PART, :].astype(jnp.float32) for part in parts]
    peak = functools.reduce(jnp.maximum, [tail[0:1] for tail in tails])
    total = jnp.zeros_like(peak)
    summed = jnp.zeros((HEAD_SIZE, 128), jnp.float32)
    for part, tail in zip(parts, tails):
        fade = jnp.exp2(tail[0:1] - peak)
        total = total + fade * (tail[1:2] + tail[2:3])
        summed = summed + fade * part[:HEAD_SIZE, :].astype(jnp.float32)
    return summed, total, peak


def kernel(
    q_hbm, k_hbm, v_hbm, ks_hbm, vs_hbm, sel_hbm, out_ref,
    kbuf, vbuf, kk, vt, qbuf, xsend, xrecv, zsend, zrecv, ks_ref, vs_ref, sel_ref, selv_ref,
    local_sem, q_send, q_recv, x_send, x_recv, z_send, z_recv,
):
    ctx = lax.axis_index("ctx")
    head = lax.axis_index("head")
    z, x = ctx // NX, ctx % NX
    y, core = head // 2, head % 2
    local_blocks = kbuf.shape[0]

    def head_at(dy, dc):
        return ((y + dy) % NY) * 2 + (core + dc) % 2

    barrier = pltpu.get_barrier_semaphore()

    def greet(to):
        pl.semaphore_signal(barrier, inc=1, device_id=to, device_id_type=MESH)

    for dz in (4, 3, 5, 2, 6):
        greet((((z + dz) % NZ) * NX + x, head))
    for step in (4, 7):
        dy, dc = turn_of(step)
        greet((ctx, head_at(dy, dc)))
    greet((z * NX + (x + 2) % NX, head))
    for step in (2, 3, 5, 6, 1):
        dy, dc = turn_of(step)
        greet((ctx, head_at(dy, dc)))
    for dx in (1, 3):
        greet((z * NX + (x + dx) % NX, head))
    for dz in (1, 7):
        greet((((z + dz) % NZ) * NX + x, head))

    local = [
        pltpu.make_async_copy(sel_hbm, selv_ref, local_sem.at[0]),
        pltpu.make_async_copy(sel_hbm, sel_ref, local_sem.at[1]),
        pltpu.make_async_copy(ks_hbm, ks_ref, local_sem.at[2]),
        pltpu.make_async_copy(vs_hbm, vs_ref, local_sem.at[3]),
        pltpu.make_async_copy(
            q_hbm.at[:, pl.ds(pl.multiple_of(head * GROUP, GROUP), GROUP), :], qbuf.at[0], local_sem.at[4]
        ),
    ]
    half = local_blocks // 2
    for k in range(2):
        part = pl.ds(k * half, half)
        local.append(pltpu.make_async_copy(k_hbm.at[part], kbuf.at[part], local_sem.at[5 + k]))
    for k in range(2):
        part = pl.ds(k * half, half)
        local.append(pltpu.make_async_copy(v_hbm.at[part], vbuf.at[part], local_sem.at[7 + k]))
    for copy in local:
        copy.start()

    pl.semaphore_wait(barrier, NSTEP - 1 + NX - 1 + NZ - 1)

    def q_remote(step):
        dy, dc = turn_of(step)
        to = head_at(dy, dc)
        return pltpu.make_async_remote_copy(
            src_ref=q_hbm.at[:, pl.ds(pl.multiple_of(to * GROUP, GROUP), GROUP), :],
            dst_ref=qbuf.at[step],
            send_sem=q_send.at[step],
            recv_sem=q_recv.at[step],
            device_id=(ctx, to),
            device_id_type=MESH,
        )

    for step in range(1, 4):
        q_remote(step).start()

    for copy in local[:4]:
        copy.wait()
    base = ctx * local_blocks
    chosen = selv_ref[...]
    first = jnp.sum((chosen < base).astype(jnp.int32))
    last = jnp.sum((chosen < base + local_blocks).astype(jnp.int32)) - 1
    factor = LOG2E / HEAD_SIZE**0.5

    for copy in local[5:]:
        copy.wait()

    def gather(turn):
        for pair in range(turn * FIRST_KC // (2 * BLK), (turn + 1) * FIRST_KC // (2 * BLK)):
            value_parts = []
            mask_parts = []
            for side in range(2):
                j = first + pair * 2 + side
                place = jnp.maximum(jnp.minimum(j, last), 0)
                block = jnp.clip(sel_ref[0, place] - base, 0, local_blocks - 1)
                key_rows = kbuf[block].astype(jnp.float32) * (ks_ref[0, block] * factor)
                high = key_rows.astype(jnp.bfloat16)
                low = (key_rows - high.astype(jnp.float32)).astype(jnp.bfloat16)
                row = (pair * 2 + side) * BLK
                kk[row : row + BLK, 0:HEAD_SIZE] = high
                kk[row : row + BLK, HEAD_SIZE : 2 * HEAD_SIZE] = low
                live = jnp.where(j <= last, 1.0, 0.0)
                value_parts.append(vbuf[block].astype(jnp.float32) * (vs_ref[0, block] * live))
                mask_parts.append(live)
            values = jnp.concatenate(value_parts, axis=0).astype(jnp.bfloat16).T
            column = pl.ds(pair * 2 * BLK, 2 * BLK)
            vt[0:HEAD_SIZE, column] = values
            lane = lax.broadcasted_iota(jnp.int32, (16, 2 * BLK), 1)
            vt[HEAD_SIZE:PART, column] = jnp.where(lane < BLK, mask_parts[0], mask_parts[1]).astype(jnp.bfloat16)

    def turned(step):
        flat = qbuf[step].reshape(ROWS, HEAD_SIZE).T
        return jnp.concatenate([flat, flat], axis=0)

    def scores_of(start, keys, queries):
        return jnp.dot(kk[start : start + keys, :], queries, preferred_element_type=jnp.float32)

    def x_remote(step, dx):
        to = (x + dx) % NX
        return pltpu.make_async_remote_copy(
            src_ref=xsend.at[step, to],
            dst_ref=xrecv.at[step, dx - 1],
            send_sem=x_send.at[step, dx - 1],
            recv_sem=x_recv.at[step, dx - 1],
            device_id=(z * NX + to, head),
            device_id_type=MESH,
        )

    def row_of(step):
        dy, dc = turn_of(step)
        return head_at(NY - dy, dc)

    def z_remote(step):
        to = row_of(step)
        slot = (z - to + NZ) % NZ - 1
        return pltpu.make_async_remote_copy(
            src_ref=zsend.at[step],
            dst_ref=zrecv.at[slot],
            send_sem=z_send.at[step],
            recv_sem=z_recv.at[slot],
            device_id=(to * NX + x, head),
            device_id_type=MESH,
        )

    def pass_on(step):
        for dx in range(1, NX):
            x_remote(step, dx).wait_recv()
        summed, total, peak = merged([xsend.at[step, x]] + [xrecv.at[step, dx] for dx in range(NX - 1)])
        summed, tail = pack(jnp.concatenate([summed, total], axis=0), peak)
        zsend[step, 0:HEAD_SIZE, :] = summed
        zsend[step, HEAD_SIZE:PART, :] = tail

        @pl.when(row_of(step) != z)
        def _():
            z_remote(step).start()

    def one_step(step, first_step):
        keys = FIRST_KC if first_step else KC
        queries = turned(step)
        if first_step:
            gather(0)
        scores = scores_of(0, keys, queries)
        peak = acc = None
        for start in range(0, KEYS, keys):
            if start + keys < KEYS:
                if first_step:
                    gather(start // keys + 1)
                coming = scores_of(start + keys, keys, queries)
            best = jnp.max(scores, axis=0, keepdims=True)
            if start > 0:
                best = jnp.maximum(peak, best)
            best = best.astype(jnp.bfloat16).astype(jnp.float32)
            prob = jnp.exp2(scores - best).astype(jnp.bfloat16)
            added = jnp.dot(vt[:, start : start + keys], prob, preferred_element_type=jnp.float32)
            acc = added if start == 0 else acc * jnp.exp2(peak - best) + added
            peak = best
            scores = coming
        summed, tail = pack(acc, peak)
        for part in range(NX):
            xsend[step, part, 0:HEAD_SIZE, :] = summed[:, part * 128 : (part + 1) * 128]
            xsend[step, part, HEAD_SIZE:PART, :] = tail[:, part * 128 : (part + 1) * 128]
        for dx in (2, 1, 3):
            x_remote(step, dx).start()

    local[4].wait()
    one_step(0, True)

    def later(step, carry):
        @pl.when(step < 5)
        def _():
            q_remote(step + 3).start()

        q_remote(step).wait_recv()
        one_step(step, False)

        @pl.when(step > 2)
        def _():
            pass_on(step - 3)

        return carry

    lax.fori_loop(1, NSTEP, later, 0)
    for step in range(NSTEP - 3, NSTEP):
        pass_on(step)

    own_y = (y - z // 2 + NY) % NY
    own_step = step_of(own_y, (core + z) % 2)
    for slot in range(NZ - 1):
        pltpu.make_async_remote_copy(
            src_ref=zsend.at[0],
            dst_ref=zrecv.at[slot],
            send_sem=z_send.at[0],
            recv_sem=z_recv.at[slot],
            device_id=(ctx, head),
            device_id_type=MESH,
        ).wait_recv()
    summed, total, _ = merged([zsend.at[own_step]] + [zrecv.at[slot] for slot in range(NZ - 1)])
    out_ref[...] = (summed / total).T.reshape(out_ref.shape).astype(out_ref.dtype)

    def finish(step, carry):
        for dx in range(1, NX):
            x_remote(step, dx).wait_send()

        @pl.when(step > 0)
        def _():
            q_remote(step).wait_send()

        @pl.when(row_of(step) != z)
        def _():
            z_remote(step).wait_send()

        return carry

    lax.fori_loop(0, NSTEP, finish, 0)


def on_device(queries, keys, values, key_block_scale, value_block_scale, selection):
    hbm = pl.BlockSpec(memory_space=pltpu.HBM)
    tokens = queries.shape[0]
    blocks = (keys.shape[1] // BLK, BLK, HEAD_SIZE)
    dma = pltpu.SemaphoreType.DMA
    return pl.pallas_call(
        kernel,
        out_shape=jax.ShapeDtypeStruct((tokens // NX, GROUP, HEAD_SIZE), jnp.bfloat16),
        in_specs=[hbm] * 6,
        out_specs=pl.BlockSpec(memory_space=pltpu.VMEM),
        scratch_shapes=[
            pltpu.VMEM(blocks, jnp.bfloat16),
            pltpu.VMEM(blocks, jnp.bfloat16),
            pltpu.VMEM((KEYS, 2 * HEAD_SIZE), jnp.bfloat16),
            pltpu.VMEM((PART, KEYS), jnp.bfloat16),
            pltpu.VMEM((NSTEP, tokens, GROUP, HEAD_SIZE), jnp.bfloat16),
            pltpu.VMEM((NSTEP, NX, PART, 128), jnp.bfloat16),
            pltpu.VMEM((NSTEP, NX - 1, PART, 128), jnp.bfloat16),
            pltpu.VMEM((NSTEP, PART, 128), jnp.bfloat16),
            pltpu.VMEM((NZ - 1, PART, 128), jnp.bfloat16),
            pltpu.SMEM((1, keys.shape[1] // BLK), jnp.float32),
            pltpu.SMEM((1, keys.shape[1] // BLK), jnp.float32),
            pltpu.SMEM(selection.shape, jnp.int32),
            pltpu.VMEM(selection.shape, jnp.int32),
            dma((9,)),
            dma((NSTEP,)),
            dma((NSTEP,)),
            dma((NSTEP, NX - 1)),
            dma((NSTEP, NX - 1)),
            dma((NSTEP,)),
            dma((NZ - 1,)),
        ],
        compiler_params=pltpu.CompilerParams(
            collective_id=0, has_side_effects=True, vmem_limit_bytes=60 << 20
        ),
    )(queries, keys.reshape(blocks), values.reshape(blocks), key_block_scale, value_block_scale, selection)


def solution(mesh):
    return jax.shard_map(
        on_device,
        mesh=mesh,
        in_specs=(
            P("head", None, None),
            P("head", "ctx", None),
            P("head", "ctx", None),
            P("head", "ctx"),
            P("head", "ctx"),
            P("head", None),
        ),
        out_specs=P("ctx", "head", None),
        check_vma=False,
    )
```
